128 devices in a mesh: row: 4 (over x), col: 16 (over z, y), depth: 2 (over core).
Axes of the slice: x: 4, y: 4, z: 4, core: 2. Of those that a mesh axis runs over, the one named last changes fastest.
Arguments:
- tokens: bfloat16 [1024, 6144], P(('depth', 'col'), 'row'), may hold values from -6 to 6
- w_in: bfloat16 [6144, 24576], P('row', 'col'), may hold values from -0.078125 to 0.078125
- w_out: bfloat16 [24576, 6144], P('col', 'row'), may hold values from -0.0390625 to 0.0390625
- cotangent: bfloat16 [1024, 6144], P(('depth', 'col'), 'row'), may hold values from -6 to 6
Outputs:
- output: bfloat16 [1024, 6144], P(('depth', 'col'), 'row')
- grad_tokens: bfloat16 [1024, 6144], P(('depth', 'col'), 'row')
- grad_w_in: bfloat16 [6144, 24576], P('row', ('col', 'depth'))
- grad_w_out: bfloat16 [24576, 6144], P(('col', 'depth'), 'row')
The draws below stay inside these ranges and needn't reach their ends.
All inputs are finite; a program needn't handle non-finite values.
Results may differ from the reference program's by a relative error of at most 0.027.
Values may be sent and summed in bfloat16 or wider, within the bound.
A program may use at most 128 MiB of HBM per device.

```python
import jax
import jax.numpy as jnp
from jax import lax

D = 6144
FF = 24576
TOKENS = 1024
N_ROW = 4
N_COL = 16


def level_of(own_key, dims, pieces, least, high):
    level, own = 1.0, jax.random.fold_in(own_key, 6)
    for axis_at, blocks in pieces:
        heights = jnp.exp(jax.random.uniform(jax.random.fold_in(own, axis_at), (blocks,), jnp.float32, least / len(pieces), high / len(pieces)))
        level = level * jnp.repeat(heights, dims[axis_at] // blocks).reshape([-1 if axis == axis_at else 1 for axis in range(len(dims))])
    return level


def centred(rng, extent, deviation, reach, shards=(), dtype=jnp.bfloat16):
    level = level_of(rng, extent, shards, -0.22, 0.18) if shards else 1.0
    entries = jax.random.normal(rng, extent, jnp.float32) * deviation * level
    return jnp.minimum(jnp.maximum(entries, -reach), reach).astype(dtype)


def setup_inputs(seed: int = 0) -> dict:
    streams_of = jax.random.split(jax.random.key(seed), 5)
    tokens = centred(streams_of[0], (TOKENS, D), 1.0, 6.0, ((0, 32), (1, 4)))
    w_in = centred(streams_of[1], (D, FF), D ** -0.5, 0.078125, ((0, 4), (1, 16)))
    w_out = centred(streams_of[2], (FF, D), FF ** -0.5, 0.0390625, ((0, 16), (1, 4)))
    cotangent = centred(streams_of[3], (TOKENS, D), 1.0, 6.0, ((0, 32), (1, 4)))
    return dict(tokens=tokens, w_in=w_in, w_out=w_out, cotangent=cotangent)


root_coeff = 0.7978845608028654
cubic_coeff = 0.044715


def gelu_value(pre_act):
    inner = root_coeff * (pre_act + cubic_coeff * pre_act * pre_act * pre_act)
    return 0.5 * pre_act * (1.0 + jnp.tanh(inner))


def gelu_slope(pre_act):
    squared = pre_act * pre_act
    tangent = jnp.tanh(root_coeff * (pre_act + cubic_coeff * squared * pre_act))
    return 0.5 * (1.0 + tangent) + 0.5 * pre_act * (1.0 - tangent * tangent) * root_coeff * (1.0 + 3.0 * cubic_coeff * squared)


def block_sum(lefthand, righthand, blocks):
    block_width = lefthand.shape[1] // blocks
    summed = jnp.zeros((lefthand.shape[0], righthand.shape[1]), jnp.float32)
    for block_index in range(blocks):
        first_col = block_index * block_width
        product = jnp.dot(lefthand[:, first_col:first_col + block_width], righthand[first_col:first_col + block_width], preferred_element_type=jnp.float32)
        rounded = lax.optimization_barrier(product.astype(jnp.bfloat16))
        summed = summed + rounded.astype(jnp.float32)
    return summed


def reference(tokens, w_in, w_out, cotangent):
    pre_hidden = block_sum(tokens, w_in, N_ROW)
    hidden = gelu_value(pre_hidden).astype(jnp.bfloat16)
    output = block_sum(hidden, w_out, N_COL).astype(jnp.bfloat16)
    grad_hidden = block_sum(cotangent, w_out.T, N_ROW)
    grad_pre = (grad_hidden * gelu_slope(pre_hidden)).astype(jnp.bfloat16)
    grad_tokens = block_sum(grad_pre, w_in.T, N_COL).astype(jnp.bfloat16)
    grad_w_in = jnp.dot(tokens.T, grad_pre, preferred_element_type=jnp.float32).astype(jnp.bfloat16)
    grad_w_out = jnp.dot(hidden.T, cotangent, preferred_element_type=jnp.float32).astype(jnp.bfloat16)
    return (output, grad_tokens, grad_w_in, grad_w_out)
```

```python
import jax
import jax.numpy as jnp
from jax import lax
from jax.experimental import pallas as pl
from jax.experimental.pallas import tpu as pltpu
from jax.sharding import PartitionSpec as P

MESH = pl.DeviceIdType.MESH
root_coeff = 0.7978845608028654
cubic_coeff = 0.044715
contract_last = (((1,), (1,)), ((), ()))
contract_first = (((0,), (0,)), ((), ()))
f32 = jnp.float32
bf16 = jnp.bfloat16
FWD, BWD = 0, 1
STEP = (0, 1, 3, 2)
TILE = 512


def gelu_value(pre_act):
    inner = root_coeff * (pre_act + cubic_coeff * pre_act * pre_act * pre_act)
    return 0.5 * pre_act * (1.0 + jnp.tanh(inner))


def gelu_slope(pre_act):
    squared = pre_act * pre_act
    tangent = jnp.tanh(root_coeff * (pre_act + cubic_coeff * squared * pre_act))
    return 0.5 * (1.0 + tangent) + 0.5 * pre_act * (1.0 - tangent * tangent) * root_coeff * (
        1.0 + 3.0 * cubic_coeff * squared
    )


def mod4(value):
    return lax.rem(value + 8, 4)


def kernel(
    tokens, w_in_hbm, w_out_hbm, cotangent,
    output, grad_tokens, grad_w_in, grad_w_out,
    w_in, w_out, slabs, other, share, passing, final, pre, act, act_other,
    share2, phase1, row_sum, phase2, out_buf, gw_in, gw_out,
    load_sem, gather_s, gather_r, scat_s, scat_r, spread_s, spread_r,
    depth_s, depth_r, col_s, col_r, store_sem,
):
    x = lax.axis_index("row")
    c = lax.axis_index("col")
    d = lax.axis_index("depth")
    z, y = c // 4, lax.rem(c, 4)
    left, right = mod4(x - 1), mod4(x + 1)
    axis_me = (z, y)

    def at_x(value):
        return {"row": value, "col": c, "depth": d}

    def at_z(value):
        return {"row": x, "col": value * 4 + y, "depth": d}

    def at_y(value):
        return {"row": x, "col": z * 4 + value, "depth": d}

    sibling = {"row": x, "col": c, "depth": 1 - d}

    def remote(src, dst, send, recv, device):
        return pltpu.make_async_remote_copy(
            src_ref=src, dst_ref=dst, send_sem=send, recv_sem=recv, device_id=device, device_id_type=MESH
        )

    sent = []

    def push(src, dst, send, recv, device):
        copy = remote(src, dst, send, recv, device)
        copy.start()
        sent.append(copy)

    def arrived(ref, send, recv):
        remote(ref, ref, send, recv, sibling).wait_recv()

    load_tok = pltpu.make_async_copy(tokens, slabs.at[FWD, z, y], load_sem.at[0])
    load_cot = pltpu.make_async_copy(cotangent, slabs.at[BWD, z, y], load_sem.at[1])
    load_in = pltpu.make_async_copy(w_in_hbm, w_in, load_sem.at[2])
    load_out = pltpu.make_async_copy(w_out_hbm, w_out, load_sem.at[3])
    for load in (load_tok, load_cot, load_in, load_out):
        load.start()

    barrier = pltpu.get_barrier_semaphore()
    peers = [at_x(left), at_x(right), sibling]
    for step in (1, 2, 3):
        peers += [at_z(mod4(z + step)), at_y(mod4(y + step))]
    for peer in peers:
        pl.semaphore_signal(barrier, inc=1, device_id=peer, device_id_type=MESH)
    pl.semaphore_wait(barrier, len(peers))

    def place(direction, k):
        return mod4(axis_me[direction] + STEP[k])

    def chunk(ref, direction, at):
        return ref.at[at] if direction == FWD else ref.at[:, at]

    def near(direction, value):
        return at_y(value) if direction == FWD else at_z(value)

    def far(direction, value):
        return at_z(value) if direction == FWD else at_y(value)

    def near_me(direction):
        return axis_me[1 - direction]

    def far_me(direction):
        return axis_me[direction]

    for direction, load in ((FWD, load_tok), (BWD, load_cot)):
        load.wait()
        own = slabs.at[direction, z, y]
        for j in (1, 2, 3):
            push(own, own, gather_s.at[direction, 0, j - 1], gather_r.at[direction, 0, j - 1],
                 near(direction, mod4(near_me(direction) + STEP[j])))

    def gather(direction, k):
        at = place(direction, k)
        blocks = chunk(slabs.at[direction], direction, at)
        if k == 0:
            for j in (1, 2, 3):
                source = mod4(near_me(direction) - STEP[j])
                block = blocks.at[source]
                arrived(block, gather_s.at[direction, 0, j - 1], gather_r.at[direction, 0, j - 1])
            for j in (1, 2, 3):
                push(blocks, blocks, gather_s.at[direction, 1, j - 1], gather_r.at[direction, 1, j - 1],
                     far(direction, mod4(far_me(direction) + STEP[j])))
        else:
            j = {1: 2, 2: 1, 3: 3}[k]
            arrived(blocks, gather_s.at[direction, 1, j - 1], gather_r.at[direction, 1, j - 1])
        push(blocks, chunk(other.at[direction], direction, at),
             depth_s.at[direction, k], depth_r.at[direction, k], sibling)

    def first_matmul(direction, k):
        at = place(direction, k)
        lhs = chunk(slabs.at[direction], direction, at)

        def tile(i, carry):
            cols = pl.ds(pl.multiple_of(i * TILE, TILE), TILE)
            rows = lhs[...].reshape(128, 1536)
            if direction == FWD:
                product = jnp.dot(rows, w_in[:, cols], preferred_element_type=f32)
            else:
                product = lax.dot_general(rows, w_out[cols, :], contract_last, preferred_element_type=f32)
            share[direction, at, :, :, cols] = product.astype(bf16).reshape(4, 32, TILE)
            return carry

        lax.fori_loop(0, 1536 // TILE, tile, 0)
        piece = lambda owner: share.at[direction, at, mod4(owner - at)]
        low, high = pl.ds(0, 16), pl.ds(16, 16)
        s = lambda n: scat_s.at[direction, k, n]
        r = lambda n: scat_r.at[direction, k, n]
        far_piece = piece(x + 2)
        push(far_piece.at[low], passing.at[direction, k, 0], s(0), r(0), at_x(right))
        push(far_piece.at[high], passing.at[direction, k, 1], s(1), r(1), at_x(left))
        push(piece(x + 1).at[high], final.at[direction, k, 0, high], s(2), r(2), at_x(right))
        push(piece(x - 1).at[low], final.at[direction, k, 1, low], s(3), r(3), at_x(left))

    def pass_on(direction, k):
        at = place(direction, k)
        low, high = pl.ds(0, 16), pl.ds(16, 16)
        for side, part, owner, n, m, to in ((0, low, x + 1, 0, 4, right), (1, high, x - 1, 1, 5, left)):
            arrived(passing.at[direction, k, side], scat_s.at[direction, k, n], scat_r.at[direction, k, n])
            mine = share.at[direction, at, mod4(owner - at)]
            total = mine[part].astype(f32) + passing[direction, k, side].astype(f32)
            mine[part] = total.astype(bf16)
            push(mine.at[part], final.at[direction, k, side, part],
                 scat_s.at[direction, k, m], scat_r.at[direction, k, m], at_x(to))

    def activate(direction, k):
        at = place(direction, k)
        low, high = pl.ds(0, 16), pl.ds(16, 16)
        for side, part, n in ((0, high, 2), (1, low, 3), (0, low, 4), (1, high, 5)):
            arrived(final.at[direction, k, side, part], scat_s.at[direction, k, n], scat_r.at[direction, k, n])
        block = mod4(x - at)
        mine = share.at[direction, at, block]
        place_z = at if direction == FWD else block
        place_y = block if direction == FWD else at
        result = act.at[direction, place_z, place_y]

        def rows(i, carry):
            part = pl.ds(pl.multiple_of(i * 16, 16), 16)
            total = mine[part].astype(f32)
            total = total + final[direction, k, 0, part].astype(f32)
            total = total + final[direction, k, 1, part].astype(f32)
            if direction == FWD:
                pre[place_z, part] = total
                result[part] = gelu_value(total).astype(bf16)
            else:
                result[part] = (total * gelu_slope(pre[place_z, part])).astype(bf16)
            return carry

        lax.fori_loop(0, 2, rows, 0)
        for n, to in ((0, right), (1, left)):
            push(result, result, spread_s.at[direction, k, n], spread_r.at[direction, k, n], at_x(to))

    def block_of(direction, at, owner):
        block = mod4(owner - at)
        return act.at[direction, at, block] if direction == FWD else act.at[direction, block, at]

    def forward_on(direction, k):
        at = place(direction, k)
        low, high = pl.ds(0, 16), pl.ds(16, 16)
        for source, part, n, to in ((x - 1, low, 0, right), (x + 1, high, 1, left)):
            block = block_of(direction, at, source)
            arrived(block, spread_s.at[direction, k, n], spread_r.at[direction, k, n])
            push(block.at[part], block.at[part], spread_s.at[direction, k, n + 2],
                 spread_r.at[direction, k, n + 2], at_x(to))

    def second_matmul(direction, k):
        at = place(direction, k)
        block = block_of(direction, at, x + 2)
        for n, part in ((2, pl.ds(0, 16)), (3, pl.ds(16, 16))):
            arrived(block.at[part], spread_s.at[direction, k, n], spread_r.at[direction, k, n])
        lhs = chunk(act.at[direction], direction, at)
        half = pl.ds(pl.multiple_of((1 - d) * 768, 128), 768)
        push(lhs.at[:, :, half], chunk(act_other.at[direction], direction, at),
             depth_s.at[direction, 4 + k], depth_r.at[direction, 4 + k], sibling)

        def tile(i, carry):
            cols = pl.ds(pl.multiple_of(i * TILE, TILE), TILE)
            rows = lhs[...].reshape(128, 1536)
            if direction == FWD:
                product = jnp.dot(rows, w_out[:, cols], preferred_element_type=f32)
            else:
                product = lax.dot_general(rows, w_in[cols, :], contract_last, preferred_element_type=f32)
            share2[direction, at, :, :, cols] = product.astype(bf16).reshape(4, 32, TILE)
            return carry

        lax.fori_loop(0, 1536 // TILE, tile, 0)
        if k:
            push(share2.at[direction, at], phase1.at[direction, k - 1],
                 col_s.at[direction, 0, k - 1], col_r.at[direction, 0, k - 1], far(direction, at))

    def sum_far(direction):
        at = place(direction, 0)
        for j in (1, 2, 3):
            arrived(phase1.at[direction, j - 1], col_s.at[direction, 0, j - 1], col_r.at[direction, 0, j - 1])

        def block(i, carry):
            total = share2[direction, at, i].astype(f32)
            for j in (0, 1, 2):
                total = total + phase1[direction, j, i].astype(f32)
            row_sum[direction, i] = total.astype(bf16)
            return carry

        lax.fori_loop(0, 4, block, 0)
        for j in (1, 2, 3):
            to = mod4(near_me(direction) + STEP[j])
            push(row_sum.at[direction, to], phase2.at[direction, j - 1],
                 col_s.at[direction, 1, j - 1], col_r.at[direction, 1, j - 1], near(direction, to))

    stores = []

    def sum_near(direction):
        for j in (1, 2, 3):
            arrived(phase2.at[direction, j - 1], col_s.at[direction, 1, j - 1], col_r.at[direction, 1, j - 1])
        total = row_sum[direction, near_me(direction)].astype(f32)
        for j in (0, 1, 2):
            total = total + phase2[direction, j].astype(f32)
        out_buf[direction] = total.astype(bf16)
        store = pltpu.make_async_copy(out_buf.at[direction], (output, grad_tokens)[direction], store_sem.at[direction])
        store.start()
        stores.append(store)

    def weight_grad(which):
        for k in range(4):
            arrived(chunk(other.at[1 - which], 1 - which, place(1 - which, k)),
                    depth_s.at[1 - which, k], depth_r.at[1 - which, k])
            arrived(chunk(act_other.at[which], which, place(which, k)),
                    depth_s.at[which, 4 + k], depth_r.at[which, 4 + k])
        width = 768 if which == FWD else 1536
        half = pl.multiple_of(d * 768, 128)
        result = gw_out if which == FWD else gw_in
        target = grad_w_out if which == FWD else grad_w_in

        def tile(i, carry):
            start = pl.multiple_of(i * 256, 256)
            rows = pl.ds(start, 256)
            if which == FWD:
                lhs = act[FWD, :, :, :, pl.ds(half + start, 256)].reshape(512, 256)
                rhs = slabs[BWD].reshape(512, 1536)
                lhs_other = act_other[FWD, :, :, :, rows].reshape(512, 256)
                rhs_other = other[BWD].reshape(512, 1536)
            else:
                lhs = slabs[FWD, :, :, :, rows].reshape(512, 256)
                rhs = act[BWD, :, :, :, pl.ds(half, 768)].reshape(512, 768)
                lhs_other = other[FWD, :, :, :, rows].reshape(512, 256)
                rhs_other = act_other[BWD].reshape(512, 768)
            product = lax.dot_general(lhs, rhs, contract_first, preferred_element_type=f32)
            product = product + lax.dot_general(lhs_other, rhs_other, contract_first, preferred_element_type=f32)
            result[rows] = product.astype(bf16)
            return carry

        lax.fori_loop(0, width // 256, tile, 0)
        store = pltpu.make_async_copy(result, target, store_sem.at[2 + which])
        store.start()
        stores.append(store)

    F, B = FWD, BWD
    gather(F, 0)
    gather(B, 0)
    load_in.wait()
    first_matmul(F, 0)
    load_out.wait()
    first_matmul(B, 0)
    pass_on(F, 0)
    gather(F, 1)
    first_matmul(F, 1)
    pass_on(B, 0)
    activate(F, 0)
    gather(B, 1)
    first_matmul(B, 1)
    pass_on(F, 1)
    forward_on(F, 0)
    gather(F, 2)
    first_matmul(F, 2)
    pass_on(B, 1)
    activate(F, 1)
    gather(B, 2)
    first_matmul(B, 2)
    pass_on(F, 2)
    forward_on(F, 1)
    second_matmul(F, 0)
    gather(F, 3)
    first_matmul(F, 3)
    pass_on(B, 2)
    activate(F, 2)
    gather(B, 3)
    first_matmul(B, 3)
    pass_on(F, 3)
    forward_on(F, 2)
    second_matmul(F, 1)
    activate(F, 3)
    pass_on(B, 3)
    activate(B, 1)
    forward_on(F, 3)
    second_matmul(F, 2)
    activate(B, 2)
    forward_on(B, 1)
    second_matmul(F, 3)
    activate(B, 3)
    forward_on(B, 2)
    second_matmul(B, 1)
    activate(B, 0)
    sum_far(F)
    forward_on(B, 3)
    second_matmul(B, 2)
    weight_grad(FWD)
    forward_on(B, 0)
    second_matmul(B, 3)
    sum_near(F)
    second_matmul(B, 0)
    sum_far(B)
    weight_grad(BWD)
    sum_near(B)
    for copy in sent:
        copy.wait_send()
    for store in stores:
        store.wait()


def body(tokens, w_in, w_out, cotangent):
    anywhere = pl.BlockSpec(memory_space=pl.ANY)
    dma = pltpu.SemaphoreType.DMA
    vmem = pltpu.VMEM
    return pl.pallas_call(
        kernel,
        out_shape=(
            jax.ShapeDtypeStruct((32, 1536), bf16),
            jax.ShapeDtypeStruct((32, 1536), bf16),
            jax.ShapeDtypeStruct((1536, 768), bf16),
            jax.ShapeDtypeStruct((768, 1536), bf16),
        ),
        in_specs=[anywhere] * 4,
        out_specs=(anywhere,) * 4,
        scratch_shapes=[
            vmem((1536, 1536), bf16),
            vmem((1536, 1536), bf16),
            vmem((2, 4, 4, 32, 1536), bf16),
            vmem((2, 4, 4, 32, 1536), bf16),
            vmem((2, 4, 4, 32, 1536), bf16),
            vmem((2, 4, 2, 16, 1536), bf16),
            vmem((2, 4, 2, 32, 1536), bf16),
            vmem((4, 32, 1536), f32),
            vmem((2, 4, 4, 32, 1536), bf16),
            vmem((2, 4, 4, 32, 768), bf16),
            vmem((2, 4, 4, 32, 1536), bf16),
            vmem((2, 3, 4, 32, 1536), bf16),
            vmem((2, 4, 32, 1536), bf16),
            vmem((2, 3, 32, 1536), bf16),
            vmem((2, 32, 1536), bf16),
            vmem((1536, 768), bf16),
            vmem((768, 1536), bf16),
            dma((4,)),
            dma((2, 2, 3)), dma((2, 2, 3)),
            dma((2, 4, 6)), dma((2, 4, 6)),
            dma((2, 4, 4)), dma((2, 4, 4)),
            dma((2, 8)), dma((2, 8)),
            dma((2, 2, 3)), dma((2, 2, 3)),
            dma((4,)),
        ],
        compiler_params=pltpu.CompilerParams(
            collective_id=1, has_side_effects=True, vmem_limit_bytes=60 * 2**20
        ),
        cost_estimate=pl.CostEstimate(flops=14_500_000_000, bytes_accessed=15_000_000, transcendentals=0),
        name="ffn_block",
    )(tokens, w_in, w_out, cotangent)


def solution(mesh):
    in_specs = (
        P(("depth", "col"), "row"),
        P("row", "col"),
        P("col", "row"),
        P(("depth", "col"), "row"),
    )
    out_specs = (
        P(("depth", "col"), "row"),
        P(("depth", "col"), "row"),
        P("row", ("col", "depth")),
        P(("col", "depth"), "row"),
    )
    return jax.shard_map(body, mesh=mesh, in_specs=in_specs, out_specs=out_specs, check_vma=False)
```

```python
import jax
import jax.numpy as jnp
from jax import lax
from jax.experimental import pallas as pl
from jax.experimental.pallas import tpu as pltpu
from jax.sharding import PartitionSpec as P

MESH = pl.DeviceIdType.MESH
root_coeff = 0.7978845608028654
cubic_coeff = 0.044715
contract_last = (((1,), (1,)), ((), ()))
contract_first = (((0,), (0,)), ((), ()))
f32 = jnp.float32
bf16 = jnp.bfloat16
FWD, BWD = 0, 1
STEP = (0, 1, 3, 2)
TILE = 512


def gelu_value(pre_act):
    inner = root_coeff * (pre_act + cubic_coeff * pre_act * pre_act * pre_act)
    return 0.5 * pre_act * (1.0 + jnp.tanh(inner))


def gelu_slope(pre_act):
    squared = pre_act * pre_act
    tangent = jnp.tanh(root_coeff * (pre_act + cubic_coeff * squared * pre_act))
    return 0.5 * (1.0 + tangent) + 0.5 * pre_act * (1.0 - tangent * tangent) * root_coeff * (
        1.0 + 3.0 * cubic_coeff * squared
    )


def mod4(value):
    return lax.rem(value + 8, 4)


def kernel(
    tokens, w_in_hbm, w_out_hbm, cotangent,
    output, grad_tokens, grad_w_in, grad_w_out,
    w_in, w_out, slabs, other, share, passing, final, pre, act, act_other,
    share2, passing1, final1, row_sum, passing2, final2, out_buf, gw_in, gw_out,
    load_sem, gather_s, gather_r, scat_s, scat_r, spread_s, spread_r,
    depth_s, depth_r, col_s, col_r, store_sem,
):
    x = lax.axis_index("row")
    c = lax.axis_index("col")
    d = lax.axis_index("depth")
    z, y = c // 4, lax.rem(c, 4)
    left, right = mod4(x - 1), mod4(x + 1)
    axis_me = (z, y)

    def at_x(value):
        return {"row": value, "col": c, "depth": d}

    def at_z(value):
        return {"row": x, "col": value * 4 + y, "depth": d}

    def at_y(value):
        return {"row": x, "col": z * 4 + value, "depth": d}

    sibling = {"row": x, "col": c, "depth": 1 - d}

    def remote(src, dst, send, recv, device):
        return pltpu.make_async_remote_copy(
            src_ref=src, dst_ref=dst, send_sem=send, recv_sem=recv, device_id=device, device_id_type=MESH
        )

    sent = []

    def push(src, dst, send, recv, device):
        copy = remote(src, dst, send, recv, device)
        copy.start()
        sent.append(copy)

    def arrived(ref, send, recv):
        remote(ref, ref, send, recv, sibling).wait_recv()

    load_tok = pltpu.make_async_copy(tokens, slabs.at[FWD, z, y], load_sem.at[0])
    load_cot = pltpu.make_async_copy(cotangent, slabs.at[BWD, z, y], load_sem.at[1])
    load_in = pltpu.make_async_copy(w_in_hbm, w_in, load_sem.at[2])
    load_out = pltpu.make_async_copy(w_out_hbm, w_out, load_sem.at[3])
    for load in (load_tok, load_cot, load_in, load_out):
        load.start()

    barrier = pltpu.get_barrier_semaphore()
    peers = [at_x(left), at_x(right), sibling]
    for step in (1, 3):
        peers += [at_z(mod4(z + step)), at_y(mod4(y + step))]
    for peer in peers:
        pl.semaphore_signal(barrier, inc=1, device_id=peer, device_id_type=MESH)
    pl.semaphore_wait(barrier, len(peers))

    def place(direction, k):
        return mod4(axis_me[direction] + STEP[k])

    def chunk(ref, direction, at):
        return ref.at[at] if direction == FWD else ref.at[:, at]

    def near(direction, value):
        return at_y(value) if direction == FWD else at_z(value)

    def far(direction, value):
        return at_z(value) if direction == FWD else at_y(value)

    def near_me(direction):
        return axis_me[1 - direction]

    def far_me(direction):
        return axis_me[direction]

    low_rows, high_rows = pl.ds(0, 16), pl.ds(16, 16)
    low_blocks, high_blocks = pl.ds(0, 2), pl.ds(2, 2)

    class Spread:
        def __init__(self, item, me, to, halves, send, recv):
            self.item, self.me, self.to, self.halves = item, me, to, halves
            self.send, self.recv = send, recv

        def part(self, offset, half):
            return self.item(mod4(self.me + offset)).at[self.halves[half]]

        def start(self):
            own, to = self.item(self.me), self.to
            for half, n, step in ((0, 0, 1), (1, 1, -1), (1, 2, 1), (0, 3, -1)):
                part = own.at[self.halves[half]]
                push(part, part, self.send(n), self.recv(n), to(mod4(self.me + step)))

        def mid(self):
            for half, n, source, step in ((0, 0, -1, 1), (1, 1, 1, -1)):
                part = self.part(source, half)
                arrived(part, self.send(n), self.recv(n))
                push(part, part, self.send(n + 4), self.recv(n + 4), self.to(mod4(self.me + step)))

        def neighbour(self, step):
            if step == 1:
                arrived(self.part(1, 0), self.send(3), self.recv(3))
            else:
                arrived(self.part(-1, 1), self.send(2), self.recv(2))

        def end(self):
            arrived(self.part(2, 0), self.send(4), self.recv(4))
            arrived(self.part(2, 1), self.send(5), self.recv(5))

    class Scatter:
        def __init__(self, piece, me, to, halves, passing, final, send, recv, add):
            self.piece, self.me, self.to, self.halves = piece, me, to, halves
            self.passing, self.final, self.send, self.recv, self.add = passing, final, send, recv, add

        def start_far(self):
            piece = self.piece(mod4(self.me + 2))
            for half, step in ((0, 1), (1, -1)):
                push(piece.at[self.halves[half]], self.passing.at[half], self.send(half), self.recv(half),
                     self.to(mod4(self.me + step)))

        def start_near(self, step):
            side = 0 if step == 1 else 1
            half = self.halves[1 - side]
            push(self.piece(mod4(self.me + step)).at[half], self.final.at[side, half],
                 self.send(2 + side), self.recv(2 + side), self.to(mod4(self.me + step)))

        def mid(self, step):
            side = 0 if step == 1 else 1
            half = self.halves[side]
            arrived(self.passing.at[side], self.send(side), self.recv(side))
            mine = self.piece(mod4(self.me + step)).at[half]
            self.add(mine, self.passing.at[side])
            push(mine, self.final.at[side, half], self.send(4 + side), self.recv(4 + side),
                 self.to(mod4(self.me + step)))

        def end(self):
            for side in (0, 1):
                arrived(self.final.at[side, self.halves[1 - side]], self.send(2 + side), self.recv(2 + side))
            for side in (0, 1):
                arrived(self.final.at[side, self.halves[side]], self.send(4 + side), self.recv(4 + side))

    def add_rows(mine, more):
        mine[...] = (mine[...].astype(f32) + more[...].astype(f32)).astype(bf16)

    def add_blocks(mine, more):
        for i in range(2):
            add_rows(mine.at[i], more.at[i])

    def ring(ref, *where):
        return lambda n: ref.at[(*where, n)]

    gather_near, gather_far, col_far, col_near = [], [], [], []
    for direction in (FWD, BWD):
        def own_line(at, direction=direction):
            return chunk(slabs.at[direction], direction, far_me(direction)).at[at]

        def whole_chunk(at, direction=direction):
            return chunk(slabs.at[direction], direction, at)

        def near_to(value, direction=direction):
            return near(direction, value)

        def far_to(value, direction=direction):
            return far(direction, value)

        def partial_chunk(at, direction=direction):
            return share2.at[direction, at]

        def summed_block(at, direction=direction):
            return row_sum.at[direction, at]

        gather_near.append(Spread(own_line, near_me(direction), near_to, (low_rows, high_rows),
                                  ring(gather_s, direction, 0), ring(gather_r, direction, 0)))
        gather_far.append(Spread(whole_chunk, far_me(direction), far_to, (low_blocks, high_blocks),
                                 ring(gather_s, direction, 1), ring(gather_r, direction, 1)))
        col_far.append(Scatter(partial_chunk, far_me(direction), far_to, (low_blocks, high_blocks),
                               passing1.at[direction], final1.at[direction],
                               ring(col_s, direction, 0), ring(col_r, direction, 0), add_blocks))
        col_near.append(Scatter(summed_block, near_me(direction), near_to, (low_rows, high_rows),
                                passing2.at[direction], final2.at[direction],
                                ring(col_s, direction, 1), ring(col_r, direction, 1), add_rows))

    def block_of(direction, at, owner):
        block = mod4(owner - at)
        return act.at[direction, at, block] if direction == FWD else act.at[direction, block, at]

    x_sum, x_spread = [[], []], [[], []]
    for direction in (FWD, BWD):
        for k in range(4):
            def piece(owner, direction=direction, at=place(direction, k)):
                return share.at[direction, at, mod4(owner - at)]

            def item(owner, direction=direction, at=place(direction, k)):
                return block_of(direction, at, owner)

            x_sum[direction].append(Scatter(
                piece, x, at_x, (low_rows, high_rows), passing.at[direction, k], final.at[direction, k],
                ring(scat_s, direction, k), ring(scat_r, direction, k), add_rows))
            x_spread[direction].append(Spread(
                item, x, at_x, (low_rows, high_rows), ring(spread_s, direction, k), ring(spread_r, direction, k)))

    def to_sibling(direction, k):
        at = place(direction, k)
        push(chunk(slabs.at[direction], direction, at), chunk(other.at[direction], direction, at),
             depth_s.at[direction, k], depth_r.at[direction, k], sibling)

    def first_matmul(direction, k):
        at = place(direction, k)
        if k == 1:
            gather_far[direction].neighbour(1)
        elif k == 2:
            gather_far[direction].neighbour(-1)
        elif k == 3:
            gather_far[direction].end()
        lhs = chunk(slabs.at[direction], direction, at)
        if k:
            to_sibling(direction, k)

        def tile(i, carry):
            cols = pl.ds(pl.multiple_of(i * TILE, TILE), TILE)
            rows = lhs[...].reshape(128, 1536)
            if direction == FWD:
                product = jnp.dot(rows, w_in[:, cols], preferred_element_type=f32)
            else:
                product = lax.dot_general(rows, w_out[cols, :], contract_last, preferred_element_type=f32)
            share[direction, at, :, :, cols] = product.astype(bf16).reshape(4, 32, TILE)
            return carry

        lax.fori_loop(0, 1536 // TILE, tile, 0)
        scatter = x_sum[direction][k]
        scatter.start_far()
        scatter.start_near(1)
        scatter.start_near(-1)

    def pass_on(direction, k):
        x_sum[direction][k].mid(1)
        x_sum[direction][k].mid(-1)

    def activate(direction, k):
        at = place(direction, k)
        x_sum[direction][k].end()
        block = mod4(x - at)
        mine = share.at[direction, at, block]
        place_z = at if direction == FWD else block
        result = block_of(direction, at, x)

        def rows(i, carry):
            part = pl.ds(pl.multiple_of(i * 16, 16), 16)
            total = mine[part].astype(f32)
            total = total + final[direction, k, 0, part].astype(f32)
            total = total + final[direction, k, 1, part].astype(f32)
            if direction == FWD:
                pre[place_z, part] = total
                result[part] = gelu_value(total).astype(bf16)
            else:
                result[part] = (total * gelu_slope(pre[place_z, part])).astype(bf16)
            return carry

        lax.fori_loop(0, 2, rows, 0)
        x_spread[direction][k].start()

    def forward_on(direction, k):
        x_spread[direction][k].mid()

    def second_matmul(direction, k):
        at = place(direction, k)
        x_spread[direction][k].neighbour(1)
        x_spread[direction][k].neighbour(-1)
        x_spread[direction][k].end()
        lhs = chunk(act.at[direction], direction, at)
        half = pl.ds(pl.multiple_of((1 - d) * 768, 128), 768)
        push(lhs.at[:, :, half], chunk(act_other.at[direction], direction, at),
             depth_s.at[direction, 4 + k], depth_r.at[direction, 4 + k], sibling)

        def tile(i, carry):
            cols = pl.ds(pl.multiple_of(i * TILE, TILE), TILE)
            rows = lhs[...].reshape(128, 1536)
            if direction == FWD:
                product = jnp.dot(rows, w_out[:, cols], preferred_element_type=f32)
            else:
                product = lax.dot_general(rows, w_in[cols, :], contract_last, preferred_element_type=f32)
            share2[direction, at, :, :, cols] = product.astype(bf16).reshape(4, 32, TILE)
            return carry

        lax.fori_loop(0, 1536 // TILE, tile, 0)
        scatter = col_far[direction]
        if k == 3:
            scatter.start_far()
        elif k:
            scatter.start_near(1 if k == 1 else -1)

    def far_mid(direction, step):
        col_far[direction].mid(step)

    def sum_far(direction):
        col_far[direction].end()
        at = place(direction, 0)

        def block(i, carry):
            total = share2[direction, at, i].astype(f32)
            for side in (0, 1):
                total = total + final1[direction, side, i].astype(f32)
            row_sum[direction, i] = total.astype(bf16)
            return carry

        lax.fori_loop(0, 4, block, 0)
        col_near[direction].start_far()
        col_near[direction].start_near(1)
        col_near[direction].start_near(-1)

    def near_mid(direction):
        col_near[direction].mid(1)
        col_near[direction].mid(-1)

    stores = []

    def sum_near(direction):
        col_near[direction].end()
        total = row_sum[direction, near_me(direction)].astype(f32)
        for side in (0, 1):
            total = total + final2[direction, side].astype(f32)
        out_buf[direction] = total.astype(bf16)
        store = pltpu.make_async_copy(out_buf.at[direction], (output, grad_tokens)[direction], store_sem.at[direction])
        store.start()
        stores.append(store)

    def grad_ready(which):
        for k in range(4):
            arrived(chunk(other.at[1 - which], 1 - which, place(1 - which, k)),
                    depth_s.at[1 - which, k], depth_r.at[1 - which, k])
            arrived(chunk(act_other.at[which], which, place(which, k)),
                    depth_s.at[which, 4 + k], depth_r.at[which, 4 + k])

    def weight_grad(which, first, last):
        width = 768 if which == FWD else 1536
        half = pl.multiple_of(d * 768, 128)
        result = gw_out if which == FWD else gw_in
        target = grad_w_out if which == FWD else grad_w_in

        def tile(i, carry):
            start = pl.multiple_of(i * 256, 256)
            rows = pl.ds(start, 256)
            if which == FWD:
                lhs = act[FWD, :, :, :, pl.ds(half + start, 256)].reshape(512, 256)
                rhs = slabs[BWD].reshape(512, 1536)
                lhs_other = act_other[FWD, :, :, :, rows].reshape(512, 256)
                rhs_other = other[BWD].reshape(512, 1536)
            else:
                lhs = slabs[FWD, :, :, :, rows].reshape(512, 256)
                rhs = act[BWD, :, :, :, pl.ds(half, 768)].reshape(512, 768)
                lhs_other = other[FWD, :, :, :, rows].reshape(512, 256)
                rhs_other = act_other[BWD].reshape(512, 768)
            product = lax.dot_general(lhs, rhs, contract_first, preferred_element_type=f32)
            product = product + lax.dot_general(lhs_other, rhs_other, contract_first, preferred_element_type=f32)
            result[rows] = product.astype(bf16)
            return carry

        lax.fori_loop(first, last, tile, 0)
        if last == width // 256:
            store = pltpu.make_async_copy(result, target, store_sem.at[2 + which])
            store.start()
            stores.append(store)

    F, B = FWD, BWD
    load_tok.wait()
    gather_near[F].start()
    load_cot.wait()
    gather_near[B].start()
    gather_near[F].mid()
    gather_near[B].mid()
    gather_near[F].neighbour(1)
    gather_near[F].neighbour(-1)
    gather_near[F].end()
    gather_far[F].start()
    to_sibling(F, 0)
    gather_near[B].neighbour(1)
    gather_near[B].neighbour(-1)
    gather_near[B].end()
    gather_far[B].start()
    to_sibling(B, 0)
    load_in.wait()
    first_matmul(F, 0)
    load_out.wait()
    first_matmul(B, 0)
    pass_on(F, 0)
    pass_on(B, 0)
    gather_far[F].mid()
    activate(F, 0)
    first_matmul(F, 1)
    first_matmul(F, 2)
    gather_far[B].mid()
    first_matmul(F, 3)
    forward_on(F, 0)
    pass_on(F, 3)
    pass_on(F, 1)
    pass_on(F, 2)
    first_matmul(B, 3)
    activate(F, 3)
    activate(F, 1)
    activate(F, 2)
    pass_on(B, 3)
    first_matmul(B, 1)
    second_matmul(F, 0)
    forward_on(F, 3)
    pass_on(B, 1)
    forward_on(F, 1)
    forward_on(F, 2)
    first_matmul(B, 2)
    second_matmul(F, 3)
    activate(B, 1)
    activate(B, 3)
    second_matmul(F, 1)
    second_matmul(F, 2)
    pass_on(B, 2)
    grad_ready(F)
    weight_grad(F, 0, 1)
    forward_on(B, 3)
    far_mid(F, 1)
    forward_on(B, 1)
    far_mid(F, -1)
    activate(B, 2)
    second_matmul(B, 3)
    forward_on(B, 2)
    second_matmul(B, 1)
    second_matmul(B, 2)
    activate(B, 0)
    far_mid(B, 1)
    weight_grad(F, 1, 2)
    far_mid(B, -1)
    forward_on(B, 0)
    weight_grad(F, 2, 3)
    second_matmul(B, 0)
    grad_ready(B)
    weight_grad(B, 0, 1)
    sum_far(F)
    sum_far(B)
    weight_grad(B, 1, 4)
    near_mid(F)
    near_mid(B)
    weight_grad(B, 4, 6)
    sum_near(F)
    sum_near(B)
    for copy in sent:
        copy.wait_send()
    for store in stores:
        store.wait()


def hand_on(*refs):
    for source, target in zip(refs[:4], refs[4:]):
        target[...] = source[...]


def body(tokens, w_in, w_out, cotangent):
    anywhere = pl.BlockSpec(memory_space=pl.ANY)
    dma = pltpu.SemaphoreType.DMA
    vmem = pltpu.VMEM
    results = pl.pallas_call(
        kernel,
        out_shape=(
            jax.ShapeDtypeStruct((32, 1536), bf16),
            jax.ShapeDtypeStruct((32, 1536), bf16),
            jax.ShapeDtypeStruct((1536, 768), bf16),
            jax.ShapeDtypeStruct((768, 1536), bf16),
        ),
        in_specs=[anywhere] * 4,
        out_specs=(anywhere,) * 4,
        scratch_shapes=[
            vmem((1536, 1536), bf16),
            vmem((1536, 1536), bf16),
            vmem((2, 4, 4, 32, 1536), bf16),
            vmem((2, 4, 4, 32, 1536), bf16),
            vmem((2, 4, 4, 32, 1536), bf16),
            vmem((2, 4, 2, 16, 1536), bf16),
            vmem((2, 4, 2, 32, 1536), bf16),
            vmem((4, 32, 1536), f32),
            vmem((2, 4, 4, 32, 1536), bf16),
            vmem((2, 4, 4, 32, 768), bf16),
            vmem((2, 4, 4, 32, 1536), bf16),
            vmem((2, 2, 2, 32, 1536), bf16),
            vmem((2, 2, 4, 32, 1536), bf16),
            vmem((2, 4, 32, 1536), bf16),
            vmem((2, 2, 16, 1536), bf16),
            vmem((2, 2, 32, 1536), bf16),
            vmem((2, 32, 1536), bf16),
            vmem((1536, 768), bf16),
            vmem((768, 1536), bf16),
            dma((4,)),
            dma((2, 2, 6)), dma((2, 2, 6)),
            dma((2, 4, 6)), dma((2, 4, 6)),
            dma((2, 4, 6)), dma((2, 4, 6)),
            dma((2, 8)), dma((2, 8)),
            dma((2, 2, 6)), dma((2, 2, 6)),
            dma((4,)),
        ],
        compiler_params=pltpu.CompilerParams(
            collective_id=1, has_side_effects=True, vmem_limit_bytes=60 * 2**20
        ),
        cost_estimate=pl.CostEstimate(flops=14_500_000_000, bytes_accessed=15_000_000, transcendentals=0),
        name="ffn_block",
    )(tokens, w_in, w_out, cotangent)
    blocks = [pl.BlockSpec((r.shape[0] // 2, r.shape[1]), lambda i: (i, 0)) for r in results]
    return pl.pallas_call(
        hand_on,
        grid=(2,),
        out_shape=tuple(jax.ShapeDtypeStruct(r.shape, r.dtype) for r in results),
        in_specs=blocks,
        out_specs=tuple(blocks),
        name="hand_on",
    )(*results)


def solution(mesh):
    in_specs = (
        P(("depth", "col"), "row"),
        P("row", "col"),
        P("col", "row"),
        P(("depth", "col"), "row"),
    )
    out_specs = (
        P(("depth", "col"), "row"),
        P(("depth", "col"), "row"),
        P("row", ("col", "depth")),
        P(("col", "depth"), "row"),
    )
    return jax.shard_map(body, mesh=mesh, in_specs=in_specs, out_specs=out_specs, check_vma=False)
```

```python
import jax
import jax.numpy as jnp
from jax import lax
from jax.experimental import pallas as pl
from jax.experimental.pallas import tpu as pltpu
from jax.sharding import PartitionSpec as P

MESH = pl.DeviceIdType.MESH
root_coeff = 0.7978845608028654
cubic_coeff = 0.044715
contract_last = (((1,), (1,)), ((), ()))
contract_first = (((0,), (0,)), ((), ()))
f32 = jnp.float32
bf16 = jnp.bfloat16
FWD, BWD = 0, 1
STEP = (0, 1, 3, 2)
TILE = 768


def gelu_value(pre_act):
    inner = root_coeff * (pre_act + cubic_coeff * pre_act * pre_act * pre_act)
    return 0.5 * pre_act * (1.0 + jnp.tanh(inner))


def gelu_slope(pre_act):
    squared = pre_act * pre_act
    tangent = jnp.tanh(root_coeff * (pre_act + cubic_coeff * squared * pre_act))
    return 0.5 * (1.0 + tangent) + 0.5 * pre_act * (1.0 - tangent * tangent) * root_coeff * (
        1.0 + 3.0 * cubic_coeff * squared
    )


def mod4(value):
    return lax.rem(value + 8, 4)


def kernel(
    tokens, w_in_hbm, w_out_hbm, cotangent,
    output, grad_tokens, grad_w_in, grad_w_out,
    w_in, w_out, slabs, other, share, passing, final, pre, act, act_other,
    share2, passing1, final1, row_sum, passing2, final2, out_buf, gw_in, gw_out,
    load_sem, gather_s, gather_r, scat_s, scat_r, spread_s, spread_r,
    depth_s, depth_r, col_s, col_r, store_sem,
):
    x = lax.axis_index("row")
    c = lax.axis_index("col")
    d = lax.axis_index("depth")
    z, y = c // 4, lax.rem(c, 4)
    left, right = mod4(x - 1), mod4(x + 1)
    axis_me = (z, y)

    def at_x(value):
        return {"row": value, "col": c, "depth": d}

    def at_z(value):
        return {"row": x, "col": value * 4 + y, "depth": d}

    def at_y(value):
        return {"row": x, "col": z * 4 + value, "depth": d}

    sibling = {"row": x, "col": c, "depth": 1 - d}

    def remote(src, dst, send, recv, device):
        return pltpu.make_async_remote_copy(
            src_ref=src, dst_ref=dst, send_sem=send, recv_sem=recv, device_id=device, device_id_type=MESH
        )

    sent = []

    def push(src, dst, send, recv, device):
        copy = remote(src, dst, send, recv, device)
        copy.start()
        sent.append(copy)

    def arrived(ref, send, recv):
        remote(ref, ref, send, recv, sibling).wait_recv()

    load_tok = pltpu.make_async_copy(tokens, slabs.at[FWD, z, y], load_sem.at[0])
    load_cot = pltpu.make_async_copy(cotangent, slabs.at[BWD, z, y], load_sem.at[1])
    load_in = pltpu.make_async_copy(w_in_hbm, w_in, load_sem.at[2])
    load_out = pltpu.make_async_copy(w_out_hbm, w_out, load_sem.at[3])
    for load in (load_tok, load_cot, load_in, load_out):
        load.start()

    barrier = pltpu.get_barrier_semaphore()
    peers = [at_x(left), at_x(right), sibling]
    for step in (1, 3):
        peers += [at_z(mod4(z + step)), at_y(mod4(y + step))]
    for peer in peers:
        pl.semaphore_signal(barrier, inc=1, device_id=peer, device_id_type=MESH)
    pl.semaphore_wait(barrier, len(peers))

    def place(direction, k):
        return mod4(axis_me[direction] + STEP[k])

    def chunk(ref, direction, at):
        return ref.at[at] if direction == FWD else ref.at[:, at]

    def near(direction, value):
        return at_y(value) if direction == FWD else at_z(value)

    def far(direction, value):
        return at_z(value) if direction == FWD else at_y(value)

    def near_me(direction):
        return axis_me[1 - direction]

    def far_me(direction):
        return axis_me[direction]

    low_rows, high_rows = pl.ds(0, 16), pl.ds(16, 16)
    low_blocks, high_blocks = pl.ds(0, 2), pl.ds(2, 2)

    class Spread:
        def __init__(self, item, me, to, halves, send, recv):
            self.item, self.me, self.to, self.halves = item, me, to, halves
            self.send, self.recv = send, recv
            self.here = set()

        def need(self, n, offset, half):
            if n not in self.here:
                self.here.add(n)
                arrived(self.part(offset, half), self.send(n), self.recv(n))

        def part(self, offset, half):
            return self.item(mod4(self.me + offset)).at[self.halves[half]]

        def start(self):
            own, to = self.item(self.me), self.to
            for half, n, step in ((0, 0, 1), (1, 1, -1), (1, 2, 1), (0, 3, -1)):
                part = own.at[self.halves[half]]
                push(part, part, self.send(n), self.recv(n), to(mod4(self.me + step)))

        def mid(self):
            for half, n, source, step in ((0, 0, -1, 1), (1, 1, 1, -1)):
                self.need(n, source, half)
                part = self.part(source, half)
                push(part, part, self.send(n + 4), self.recv(n + 4), self.to(mod4(self.me + step)))

        def neighbour(self, step):
            for n, half in ((1, 1), (3, 0)) if step == 1 else ((0, 0), (2, 1)):
                self.need(n, step, half)

        def end(self):
            self.need(4, 2, 0)
            self.need(5, 2, 1)

    class Scatter:
        def __init__(self, piece, me, to, halves, passing, final, send, recv, add):
            self.piece, self.me, self.to, self.halves = piece, me, to, halves
            self.passing, self.final, self.send, self.recv, self.add = passing, final, send, recv, add

        def start_far(self):
            piece = self.piece(mod4(self.me + 2))
            for half, step in ((0, 1), (1, -1)):
                push(piece.at[self.halves[half]], self.passing.at[half], self.send(half), self.recv(half),
                     self.to(mod4(self.me + step)))

        def start_near(self, step):
            side = 0 if step == 1 else 1
            half = self.halves[1 - side]
            push(self.piece(mod4(self.me + step)).at[half], self.final.at[side, half],
                 self.send(2 + side), self.recv(2 + side), self.to(mod4(self.me + step)))

        def mid(self, step):
            side = 0 if step == 1 else 1
            half = self.halves[side]
            arrived(self.passing.at[side], self.send(side), self.recv(side))
            mine = self.piece(mod4(self.me + step)).at[half]
            self.add(mine, self.passing.at[side])
            push(mine, self.final.at[side, half], self.send(4 + side), self.recv(4 + side),
                 self.to(mod4(self.me + step)))

        def end(self):
            for side in (0, 1):
                arrived(self.final.at[side, self.halves[1 - side]], self.send(2 + side), self.recv(2 + side))
            for side in (0, 1):
                arrived(self.final.at[side, self.halves[side]], self.send(4 + side), self.recv(4 + side))

    def add_rows(mine, more):
        mine[...] = (mine[...].astype(f32) + more[...].astype(f32)).astype(bf16)

    def add_blocks(mine, more):
        for i in range(2):
            add_rows(mine.at[i], more.at[i])

    def ring(ref, *where):
        return lambda n: ref.at[(*where, n)]

    gather_near, gather_far, col_far, col_near = [], [], [], []
    for direction in (FWD, BWD):
        def own_line(at, direction=direction):
            return chunk(slabs.at[direction], direction, far_me(direction)).at[at]

        def near_to(value, direction=direction):
            return near(direction, value)

        def far_to(value, direction=direction):
            return far(direction, value)

        def partial_chunk(at, direction=direction):
            return share2.at[direction, at]

        def summed_block(at, direction=direction):
            return row_sum.at[direction, at]

        gather_near.append(Spread(own_line, near_me(direction), near_to, (low_rows, high_rows),
                                  ring(gather_s, direction, 0), ring(gather_r, direction, 0)))
        lines = []
        for j in range(4):
            def far_line(at, direction=direction, block=mod4(near_me(direction) + STEP[j])):
                return chunk(slabs.at[direction], direction, at).at[block]

            lines.append(Spread(far_line, far_me(direction), far_to, (low_rows, high_rows),
                                ring(gather_s, direction, 1 + j), ring(gather_r, direction, 1 + j)))
        gather_far.append(lines)
        col_far.append(Scatter(partial_chunk, far_me(direction), far_to, (low_blocks, high_blocks),
                               passing1.at[direction], final1.at[direction],
                               ring(col_s, direction, 0), ring(col_r, direction, 0), add_blocks))
        col_near.append(Scatter(summed_block, near_me(direction), near_to, (low_rows, high_rows),
                                passing2.at[direction], final2.at[direction],
                                ring(col_s, direction, 1), ring(col_r, direction, 1), add_rows))

    def block_of(direction, at, owner):
        block = mod4(owner - at)
        return act.at[direction, at, block] if direction == FWD else act.at[direction, block, at]

    x_sum, x_spread = [[], []], [[], []]
    for direction in (FWD, BWD):
        for k in range(4):
            def piece(owner, direction=direction, at=place(direction, k)):
                return share.at[direction, at, mod4(owner - at)]

            def item(owner, direction=direction, at=place(direction, k)):
                return block_of(direction, at, owner)

            x_sum[direction].append(Scatter(
                piece, x, at_x, (low_rows, high_rows), passing.at[direction, k], final.at[direction, k],
                ring(scat_s, direction, k), ring(scat_r, direction, k), add_rows))
            x_spread[direction].append(Spread(
                item, x, at_x, (low_rows, high_rows), ring(spread_s, direction, k), ring(spread_r, direction, k)))

    def to_sibling(direction, k):
        at = place(direction, k)
        push(chunk(slabs.at[direction], direction, at), chunk(other.at[direction], direction, at),
             depth_s.at[direction, k], depth_r.at[direction, k], sibling)

    def first_matmul(direction, k):
        at = place(direction, k)
        for line in gather_far[direction]:
            if k == 1:
                line.neighbour(1)
            elif k == 2:
                line.neighbour(-1)
            elif k == 3:
                line.end()
        lhs = chunk(slabs.at[direction], direction, at)
        if k:
            to_sibling(direction, k)

        def tile(i, carry):
            cols = pl.ds(pl.multiple_of(i * TILE, TILE), TILE)
            rows = lhs[...].reshape(128, 1536)
            if direction == FWD:
                product = jnp.dot(rows, w_in[:, cols], preferred_element_type=f32)
            else:
                product = lax.dot_general(rows, w_out[cols, :], contract_last, preferred_element_type=f32)
            share[direction, at, :, :, cols] = product.astype(bf16).reshape(4, 32, TILE)
            return carry

        lax.fori_loop(0, 1536 // TILE, tile, 0)
        scatter = x_sum[direction][k]
        scatter.start_far()
        scatter.start_near(1)
        scatter.start_near(-1)

    def pass_on(direction, k):
        x_sum[direction][k].mid(1)
        x_sum[direction][k].mid(-1)

    def activate(direction, k):
        at = place(direction, k)
        x_sum[direction][k].end()
        block = mod4(x - at)
        mine = share.at[direction, at, block]
        place_z = at if direction == FWD else block
        result = block_of(direction, at, x)

        def rows(i, carry):
            part = pl.ds(pl.multiple_of(i * 16, 16), 16)
            total = mine[part].astype(f32)
            total = total + final[direction, k, 0, part].astype(f32)
            total = total + final[direction, k, 1, part].astype(f32)
            if direction == FWD:
                pre[place_z, part] = total
                result[part] = gelu_value(total).astype(bf16)
            else:
                result[part] = (total * gelu_slope(pre[place_z, part])).astype(bf16)
            return carry

        lax.fori_loop(0, 2, rows, 0)
        x_spread[direction][k].start()

    def forward_on(direction, k):
        x_spread[direction][k].mid()

    def second_matmul(direction, k):
        at = place(direction, k)
        x_spread[direction][k].neighbour(1)
        x_spread[direction][k].neighbour(-1)
        x_spread[direction][k].end()
        if k == 0 and direction == BWD:
            col_far[direction].end()
        lhs = chunk(act.at[direction], direction, at)
        half = pl.ds(pl.multiple_of((1 - d) * 768, 128), 768)
        push(lhs.at[:, :, half], chunk(act_other.at[direction], direction, at),
             depth_s.at[direction, 4 + k], depth_r.at[direction, 4 + k], sibling)

        def tile(i, carry):
            cols = pl.ds(pl.multiple_of(i * TILE, TILE), TILE)
            rows = lhs[...].reshape(128, 1536)
            if direction == FWD:
                product = jnp.dot(rows, w_out[:, cols], preferred_element_type=f32)
            else:
                product = lax.dot_general(rows, w_in[cols, :], contract_last, preferred_element_type=f32)
            if k == 0 and direction == BWD:
                product = product.reshape(4, 32, TILE)
                for side in (0, 1):
                    product = product + final1[direction, side, :, :, cols].astype(f32)
                row_sum[direction, :, :, cols] = product.astype(bf16)
                return carry
            share2[direction, at, :, :, cols] = product.astype(bf16).reshape(4, 32, TILE)
            return carry

        lax.fori_loop(0, 1536 // TILE, tile, 0)
        scatter = col_far[direction]
        if k == 3:
            scatter.start_far()
        elif k:
            scatter.start_near(1 if k == 1 else -1)

    def far_mid(direction, step):
        col_far[direction].mid(step)

    def sum_far(direction):
        at = place(direction, 0)

        def block(i, carry):
            total = share2[direction, at, i].astype(f32)
            for side in (0, 1):
                total = total + final1[direction, side, i].astype(f32)
            row_sum[direction, i] = total.astype(bf16)
            return carry

        if direction == FWD:
            col_far[direction].end()
            lax.fori_loop(0, 4, block, 0)
        col_near[direction].start_far()
        col_near[direction].start_near(1)
        col_near[direction].start_near(-1)

    def near_mid(direction):
        col_near[direction].mid(1)
        col_near[direction].mid(-1)

    stores = []

    def sum_near(direction):
        col_near[direction].end()
        total = row_sum[direction, near_me(direction)].astype(f32)
        for side in (0, 1):
            total = total + final2[direction, side].astype(f32)
        out_buf[direction] = total.astype(bf16)
        store = pltpu.make_async_copy(out_buf.at[direction], (output, grad_tokens)[direction], store_sem.at[direction])
        store.start()
        stores.append(store)

    def grad_ready(which):
        for k in range(4):
            arrived(chunk(other.at[1 - which], 1 - which, place(1 - which, k)),
                    depth_s.at[1 - which, k], depth_r.at[1 - which, k])
            arrived(chunk(act_other.at[which], which, place(which, k)),
                    depth_s.at[which, 4 + k], depth_r.at[which, 4 + k])

    def weight_grad(which, first, last):
        width = 768 if which == FWD else 1536
        half = pl.multiple_of(d * 768, 128)
        result = gw_out if which == FWD else gw_in
        target = grad_w_out if which == FWD else grad_w_in

        def tile(i, carry):
            start = pl.multiple_of(i * 256, 256)
            rows = pl.ds(start, 256)
            if which == FWD:
                lhs = act[FWD, :, :, :, pl.ds(half + start, 256)].reshape(512, 256)
                rhs = slabs[BWD].reshape(512, 1536)
                lhs_other = act_other[FWD, :, :, :, rows].reshape(512, 256)
                rhs_other = other[BWD].reshape(512, 1536)
            else:
                lhs = slabs[FWD, :, :, :, rows].reshape(512, 256)
                rhs = act[BWD, :, :, :, pl.ds(half, 768)].reshape(512, 768)
                lhs_other = other[FWD, :, :, :, rows].reshape(512, 256)
                rhs_other = act_other[BWD].reshape(512, 768)
            product = lax.dot_general(lhs, rhs, contract_first, preferred_element_type=f32)
            product = product + lax.dot_general(lhs_other, rhs_other, contract_first, preferred_element_type=f32)
            result[rows] = product.astype(bf16)
            return carry

        lax.fori_loop(first, last, tile, 0)
        if last == width // 256:
            store = pltpu.make_async_copy(result, target, store_sem.at[2 + which])
            store.start()
            stores.append(store)

    F, B = FWD, BWD
    load_tok.wait()
    gather_near[F].start()
    load_cot.wait()
    gather_near[B].start()
    gather_far[B][0].start()
    gather_far[F][0].start()
    gather_near[B].mid()
    gather_near[F].mid()
    gather_near[B].neighbour(1)
    gather_near[B].neighbour(-1)
    gather_near[F].neighbour(1)
    gather_near[F].neighbour(-1)
    gather_far[F][1].start()
    gather_far[F][2].start()
    gather_far[B][1].start()
    gather_far[B][2].start()
    gather_near[F].end()
    to_sibling(F, 0)
    gather_near[B].end()
    to_sibling(B, 0)
    load_in.wait()
    first_matmul(F, 0)
    gather_far[B][3].start()
    gather_far[F][3].start()
    load_out.wait()
    first_matmul(B, 0)
    gather_far[B][2].mid()
    gather_far[F][0].mid()
    gather_far[B][0].mid()
    gather_far[F][1].mid()
    gather_far[F][2].mid()
    pass_on(F, 0)
    gather_far[B][3].mid()
    gather_far[F][3].mid()
    gather_far[B][1].mid()
    first_matmul(F, 1)
    first_matmul(B, 1)
    first_matmul(F, 3)
    first_matmul(F, 2)
    first_matmul(B, 2)
    pass_on(B, 1)
    pass_on(F, 1)
    pass_on(F, 3)
    pass_on(F, 2)
    pass_on(B, 2)
    first_matmul(B, 3)
    activate(F, 1)
    pass_on(B, 3)
    activate(F, 0)
    activate(F, 3)
    activate(F, 2)
    activate(B, 3)
    activate(B, 1)
    forward_on(B, 3)
    forward_on(F, 3)
    activate(B, 2)
    forward_on(B, 1)
    second_matmul(B, 3)
    forward_on(B, 2)
    pass_on(B, 0)
    forward_on(F, 1)
    forward_on(F, 2)
    second_matmul(F, 3)
    second_matmul(B, 1)
    second_matmul(B, 2)
    forward_on(F, 0)
    activate(B, 0)
    second_matmul(F, 1)
    second_matmul(F, 2)
    far_mid(B, -1)
    far_mid(F, -1)
    far_mid(F, 1)
    far_mid(B, 1)
    forward_on(B, 0)
    second_matmul(F, 0)
    grad_ready(F)
    weight_grad(F, 0, 2)
    second_matmul(B, 0)
    sum_far(B)
    grad_ready(B)
    weight_grad(B, 0, 1)
    sum_far(F)
    weight_grad(B, 1, 3)
    near_mid(B)
    weight_grad(B, 3, 4)
    near_mid(F)
    weight_grad(B, 4, 5)
    weight_grad(F, 2, 3)
    sum_near(B)
    weight_grad(B, 5, 6)
    sum_near(F)
    for copy in sent:
        copy.wait_send()
    for store in stores:
        store.wait()


def hand_on(*refs):
    for source, target in zip(refs[:4], refs[4:]):
        target[...] = source[...]


def body(tokens, w_in, w_out, cotangent):
    anywhere = pl.BlockSpec(memory_space=pl.ANY)
    dma = pltpu.SemaphoreType.DMA
    vmem = pltpu.VMEM
    results = pl.pallas_call(
        kernel,
        out_shape=(
            jax.ShapeDtypeStruct((32, 1536), bf16),
            jax.ShapeDtypeStruct((32, 1536), bf16),
            jax.ShapeDtypeStruct((1536, 768), bf16),
            jax.ShapeDtypeStruct((768, 1536), bf16),
        ),
        in_specs=[anywhere] * 4,
        out_specs=(anywhere,) * 4,
        scratch_shapes=[
            vmem((1536, 1536), bf16),
            vmem((1536, 1536), bf16),
            vmem((2, 4, 4, 32, 1536), bf16),
            vmem((2, 4, 4, 32, 1536), bf16),
            vmem((2, 4, 4, 32, 1536), bf16),
            vmem((2, 4, 2, 16, 1536), bf16),
            vmem((2, 4, 2, 32, 1536), bf16),
            vmem((4, 32, 1536), f32),
            vmem((2, 4, 4, 32, 1536), bf16),
            vmem((2, 4, 4, 32, 768), bf16),
            vmem((2, 4, 4, 32, 1536), bf16),
            vmem((2, 2, 2, 32, 1536), bf16),
            vmem((2, 2, 4, 32, 1536), bf16),
            vmem((2, 4, 32, 1536), bf16),
            vmem((2, 2, 16, 1536), bf16),
            vmem((2, 2, 32, 1536), bf16),
            vmem((2, 32, 1536), bf16),
            vmem((1536, 768), bf16),
            vmem((768, 1536), bf16),
            dma((4,)),
            dma((2, 5, 6)), dma((2, 5, 6)),
            dma((2, 4, 6)), dma((2, 4, 6)),
            dma((2, 4, 6)), dma((2, 4, 6)),
            dma((2, 8)), dma((2, 8)),
            dma((2, 2, 6)), dma((2, 2, 6)),
            dma((4,)),
        ],
        compiler_params=pltpu.CompilerParams(
            collective_id=1, has_side_effects=True, vmem_limit_bytes=60 * 2**20
        ),
        cost_estimate=pl.CostEstimate(flops=14_500_000_000, bytes_accessed=15_000_000, transcendentals=0),
        name="ffn_block",
    )(tokens, w_in, w_out, cotangent)
    blocks = [pl.BlockSpec((r.shape[0] // 2, r.shape[1]), lambda i: (i, 0)) for r in results]
    return pl.pallas_call(
        hand_on,
        grid=(2,),
        out_shape=tuple(jax.ShapeDtypeStruct(r.shape, r.dtype) for r in results),
        in_specs=blocks,
        out_specs=tuple(blocks),
        name="hand_on",
    )(*results)


def solution(mesh):
    in_specs = (
        P(("depth", "col"), "row"),
        P("row", "col"),
        P("col", "row"),
        P(("depth", "col"), "row"),
    )
    out_specs = (
        P(("depth", "col"), "row"),
        P(("depth", "col"), "row"),
        P("row", ("col", "depth")),
        P(("col", "depth"), "row"),
    )
    return jax.shard_map(body, mesh=mesh, in_specs=in_specs, out_specs=out_specs, check_vma=False)
```

```python
import jax
import jax.numpy as jnp
from jax import lax
from jax.experimental import pallas as pl
from jax.experimental.pallas import tpu as pltpu
from jax.sharding import PartitionSpec as P

MESH = pl.DeviceIdType.MESH
root_coeff = 0.7978845608028654
cubic_coeff = 0.044715
contract_first = (((0,), (0,)), ((), ()))
f32 = jnp.float32
bf16 = jnp.bfloat16
FWD, BWD = 0, 1
STEP = (0, 1, 3, 2)
TILE = 768


def gelu_value(pre_act):
    inner = root_coeff * (pre_act + cubic_coeff * pre_act * pre_act * pre_act)
    return 0.5 * pre_act * (1.0 + jnp.tanh(inner))


def gelu_slope(pre_act):
    squared = pre_act * pre_act
    tangent = jnp.tanh(root_coeff * (pre_act + cubic_coeff * squared * pre_act))
    return 0.5 * (1.0 + tangent) + 0.5 * pre_act * (1.0 - tangent * tangent) * root_coeff * (
        1.0 + 3.0 * cubic_coeff * squared
    )


def mod4(value):
    return lax.rem(value + 8, 4)


def kernel(
    tokens, w_in_hbm, w_out_hbm, cotangent,
    output, grad_tokens, grad_w_in, grad_w_out,
    w_in, w_out, w_in_t, w_out_t, slabs, other, share, passing, final, pre, act, act_other,
    share2, passing1, final1, row_sum, passing2, final2, out_buf, gw_in, gw_out,
    load_sem, gather_s, gather_r, scat_s, scat_r, spread_s, spread_r,
    depth_s, depth_r, col_s, col_r, store_sem, grad_sem,
):
    x = lax.axis_index("row")
    c = lax.axis_index("col")
    d = lax.axis_index("depth")
    z, y = c // 4, lax.rem(c, 4)
    left, right = mod4(x - 1), mod4(x + 1)
    axis_me = (z, y)

    def at_x(value):
        return {"row": value, "col": c, "depth": d}

    def at_z(value):
        return {"row": x, "col": value * 4 + y, "depth": d}

    def at_y(value):
        return {"row": x, "col": z * 4 + value, "depth": d}

    sibling = {"row": x, "col": c, "depth": 1 - d}

    def remote(src, dst, send, recv, device):
        return pltpu.make_async_remote_copy(
            src_ref=src, dst_ref=dst, send_sem=send, recv_sem=recv, device_id=device, device_id_type=MESH
        )

    sent = []

    def push(src, dst, send, recv, device):
        copy = remote(src, dst, send, recv, device)
        copy.start()
        sent.append(copy)

    def arrived(ref, send, recv):
        remote(ref, ref, send, recv, sibling).wait_recv()

    load_tok = pltpu.make_async_copy(tokens, slabs.at[FWD, z, y], load_sem.at[0])
    load_cot = pltpu.make_async_copy(cotangent, slabs.at[BWD, z, y], load_sem.at[1])
    load_in = pltpu.make_async_copy(w_in_hbm, w_in, load_sem.at[2])
    load_out = pltpu.make_async_copy(w_out_hbm, w_out, load_sem.at[3])
    for load in (load_tok, load_cot, load_in, load_out):
        load.start()

    barrier = pltpu.get_barrier_semaphore()
    peers = [at_x(left), at_x(right), sibling]
    for step in (1, 2, 3):
        peers += [at_z(mod4(z + step)), at_y(mod4(y + step))]
    for peer in peers:
        pl.semaphore_signal(barrier, inc=1, device_id=peer, device_id_type=MESH)
    pl.semaphore_wait(barrier, len(peers))

    def place(direction, k):
        return mod4(axis_me[direction] + STEP[k])

    def chunk(ref, direction, at):
        return ref.at[at] if direction == FWD else ref.at[:, at]

    def near(direction, value):
        return at_y(value) if direction == FWD else at_z(value)

    def far(direction, value):
        return at_z(value) if direction == FWD else at_y(value)

    def near_me(direction):
        return axis_me[1 - direction]

    def far_me(direction):
        return axis_me[direction]

    low_rows, high_rows = pl.ds(0, 16), pl.ds(16, 16)
    low_blocks, high_blocks = pl.ds(0, 2), pl.ds(2, 2)

    class Spread:
        def __init__(self, item, me, to, halves, send, recv, direct=False):
            self.direct = direct
            self.item, self.me, self.to, self.halves = item, me, to, halves
            self.send, self.recv = send, recv
            self.here = set()

        def need(self, n, offset, half):
            if n not in self.here:
                self.here.add(n)
                arrived(self.part(offset, half), self.send(n), self.recv(n))

        def part(self, offset, half):
            return self.item(mod4(self.me + offset)).at[self.halves[half]]

        def start(self):
            own, to = self.item(self.me), self.to
            for half, n, step in ((0, 0, 1), (1, 1, -1), (1, 2, 1), (0, 3, -1)):
                part = own.at[self.halves[half]]
                push(part, part, self.send(n), self.recv(n), to(mod4(self.me + step)))
            if self.direct:
                for half in (0, 1):
                    part = own.at[self.halves[half]]
                    push(part, part, self.send(4 + half), self.recv(4 + half), to(mod4(self.me + 2)))

        def mid(self):
            if self.direct:
                return
            for half, n, source, step in ((0, 0, -1, 1), (1, 1, 1, -1)):
                self.need(n, source, half)
                part = self.part(source, half)
                push(part, part, self.send(n + 4), self.recv(n + 4), self.to(mod4(self.me + step)))

        def neighbour(self, step):
            for n, half in ((1, 1), (3, 0)) if step == 1 else ((0, 0), (2, 1)):
                self.need(n, step, half)

        def end(self):
            self.need(4, 2, 0)
            self.need(5, 2, 1)

    class Scatter:
        def __init__(self, piece, me, to, halves, passing, final, send, recv, add, direct=False):
            self.direct = direct
            self.piece, self.me, self.to, self.halves = piece, me, to, halves
            self.passing, self.final, self.send, self.recv, self.add = passing, final, send, recv, add

        def start_far(self):
            piece = self.piece(mod4(self.me + 2))
            for half, step in ((0, 1), (1, -1)):
                push(piece.at[self.halves[half]], self.passing.at[half], self.send(half), self.recv(half),
                     self.to(mod4(self.me + (2 if self.direct else step))))

        def start_near(self, step):
            side = 0 if step == 1 else 1
            half = self.halves[1 - side]
            push(self.piece(mod4(self.me + step)).at[half], self.final.at[side, half],
                 self.send(2 + side), self.recv(2 + side), self.to(mod4(self.me + step)))
            if self.direct:
                half = self.halves[side]
                push(self.piece(mod4(self.me + step)).at[half], self.final.at[side, half],
                     self.send(4 + side), self.recv(4 + side), self.to(mod4(self.me + step)))

        def mid(self, step):
            if self.direct:
                return
            side = 0 if step == 1 else 1
            half = self.halves[side]
            arrived(self.passing.at[side], self.send(side), self.recv(side))
            mine = self.piece(mod4(self.me + step)).at[half]
            self.add(mine, self.passing.at[side])
            push(mine, self.final.at[side, half], self.send(4 + side), self.recv(4 + side),
                 self.to(mod4(self.me + step)))

        def end(self):
            if self.direct:
                for half in (0, 1):
                    arrived(self.passing.at[half], self.send(half), self.recv(half))
            for side in (0, 1):
                arrived(self.final.at[side, self.halves[1 - side]], self.send(2 + side), self.recv(2 + side))
            for side in (0, 1):
                arrived(self.final.at[side, self.halves[side]], self.send(4 + side), self.recv(4 + side))

    def add_rows(mine, more):
        mine[...] = (mine[...].astype(f32) + more[...].astype(f32)).astype(bf16)

    def add_blocks(mine, more):
        for i in range(2):
            add_rows(mine.at[i], more.at[i])

    def ring(ref, *where):
        return lambda n: ref.at[(*where, n)]

    gather_near, gather_far, col_far, col_near = [], [], [], []
    for direction in (FWD, BWD):
        def own_line(at, direction=direction):
            return chunk(slabs.at[direction], direction, far_me(direction)).at[at]

        def near_to(value, direction=direction):
            return near(direction, value)

        def far_to(value, direction=direction):
            return far(direction, value)

        def partial_chunk(at, direction=direction):
            return share2.at[direction, at]

        gather_near.append(Spread(own_line, near_me(direction), near_to, (low_rows, high_rows),
                                  ring(gather_s, direction, 0), ring(gather_r, direction, 0), True))
        lines = []
        for j in range(4):
            def far_line(at, direction=direction, block=mod4(near_me(direction) + STEP[j])):
                return chunk(slabs.at[direction], direction, at).at[block]

            lines.append(Spread(far_line, far_me(direction), far_to, (low_rows, high_rows),
                                ring(gather_s, direction, 1 + j), ring(gather_r, direction, 1 + j)))
        gather_far.append(lines)
        col_far.append(Scatter(partial_chunk, far_me(direction), far_to, (low_blocks, high_blocks),
                               passing1.at[direction], final1.at[direction],
                               ring(col_s, direction, 0), ring(col_r, direction, 0), add_blocks))
        halves = []
        for h in (0, 1):
            def summed_block(at, direction=direction, h=h):
                return row_sum.at[direction, h, at]

            halves.append(Scatter(summed_block, near_me(direction), near_to, (low_rows, high_rows),
                                  passing2.at[direction, h], final2.at[direction, h],
                                  ring(col_s, direction, 1 + h), ring(col_r, direction, 1 + h), add_rows, True))
        col_near.append(halves)

    def block_of(direction, at, owner):
        block = mod4(owner - at)
        return act.at[direction, at, block] if direction == FWD else act.at[direction, block, at]

    x_sum, x_spread = [[], []], [[], []]
    for direction in (FWD, BWD):
        for k in range(4):
            def piece(owner, direction=direction, at=place(direction, k)):
                return share.at[direction, at, mod4(owner - at)]

            def item(owner, direction=direction, at=place(direction, k)):
                return block_of(direction, at, owner)

            x_sum[direction].append(Scatter(
                piece, x, at_x, (low_rows, high_rows), passing.at[direction, k], final.at[direction, k],
                ring(scat_s, direction, k), ring(scat_r, direction, k), add_rows))
            x_spread[direction].append(Spread(
                item, x, at_x, (low_rows, high_rows), ring(spread_s, direction, k), ring(spread_r, direction, k)))

    def turn(direction, i):
        rows = pl.ds(i * 512, 512)
        if direction == FWD:
            w_in_t[:, rows] = w_in[rows, :].T
        else:
            w_out_t[:, rows] = w_out[rows, :].T

    far_mids, at_once = [0, 0], [False, False]

    def to_sibling(direction, k):
        at = place(direction, k)
        push(chunk(slabs.at[direction], direction, at), chunk(other.at[direction], direction, at),
             depth_s.at[direction, k], depth_r.at[direction, k], sibling)

    def first_matmul(direction, k):
        at = place(direction, k)
        for line in gather_far[direction]:
            if k == 1:
                line.neighbour(1)
            elif k == 2:
                line.neighbour(-1)
            elif k == 3:
                line.end()
        lhs = chunk(slabs.at[direction], direction, at)
        if k:
            to_sibling(direction, k)

        def tile(i, carry):
            cols = pl.ds(pl.multiple_of(i * TILE, TILE), TILE)
            rows = lhs[...].reshape(128, 1536)
            if direction == FWD:
                product = jnp.dot(rows, w_in[:, cols], preferred_element_type=f32)
            else:
                product = jnp.dot(rows, w_out_t[:, cols], preferred_element_type=f32)
            share[direction, at, :, :, cols] = product.astype(bf16).reshape(4, 32, TILE)
            return carry

        lax.fori_loop(0, 1536 // TILE, tile, 0)
        scatter = x_sum[direction][k]
        scatter.start_far()
        scatter.start_near(1)
        scatter.start_near(-1)

    def pass_on(direction, k):
        x_sum[direction][k].mid(1)
        x_sum[direction][k].mid(-1)

    def activate(direction, k):
        at = place(direction, k)
        x_sum[direction][k].end()
        block = mod4(x - at)
        mine = share.at[direction, at, block]
        place_z = at if direction == FWD else block
        result = block_of(direction, at, x)

        def rows(i, carry):
            part = pl.ds(pl.multiple_of(i * 16, 16), 16)
            total = mine[part].astype(f32)
            total = total + final[direction, k, 0, part].astype(f32)
            total = total + final[direction, k, 1, part].astype(f32)
            if direction == FWD:
                pre[place_z, part] = total
                result[part] = gelu_value(total).astype(bf16)
            else:
                result[part] = (total * gelu_slope(pre[place_z, part])).astype(bf16)
            return carry

        lax.fori_loop(0, 2, rows, 0)
        x_spread[direction][k].start()

    def forward_on(direction, k):
        x_spread[direction][k].mid()

    def second_matmul(direction, k):
        at = place(direction, k)
        x_spread[direction][k].neighbour(1)
        x_spread[direction][k].neighbour(-1)
        x_spread[direction][k].end()
        if k == 0 and far_mids[direction] == 2:
            col_far[direction].end()
            at_once[direction] = True
        lhs = chunk(act.at[direction], direction, at)
        half = pl.ds(pl.multiple_of((1 - d) * 768, 128), 768)
        push(lhs.at[:, :, half], chunk(act_other.at[direction], direction, at),
             depth_s.at[direction, 4 + k], depth_r.at[direction, 4 + k], sibling)

        def tile(i, carry):
            cols = pl.ds(pl.multiple_of(i * TILE, TILE), TILE)
            rows = lhs[...].reshape(128, 1536)
            if direction == FWD:
                product = jnp.dot(rows, w_out[:, cols], preferred_element_type=f32)
            else:
                product = jnp.dot(rows, w_in_t[:, cols], preferred_element_type=f32)
            if k == 0 and at_once[direction]:
                product = product.reshape(4, 32, TILE)
                for side in (0, 1):
                    product = product + final1[direction, side, :, :, cols].astype(f32)
                row_sum[direction, i] = product.astype(bf16)
                return carry
            share2[direction, at, :, :, cols] = product.astype(bf16).reshape(4, 32, TILE)
            return carry

        if k == 0 and at_once[direction]:
            for h in (0, 1):
                lax.fori_loop(h, h + 1, tile, 0)
                near_start(direction, h)
            return
        lax.fori_loop(0, 1536 // TILE, tile, 0)
        scatter = col_far[direction]
        if k == 3:
            scatter.start_far()
        elif k:
            scatter.start_near(1 if k == 1 else -1)

    def far_mid(direction, step):
        col_far[direction].mid(step)
        far_mids[direction] += 1

    def near_start(direction, h):
        col_near[direction][h].start_far()
        col_near[direction][h].start_near(1)
        col_near[direction][h].start_near(-1)

    def sum_far(direction):
        if at_once[direction]:
            return
        col_far[direction].end()
        at = place(direction, 0)
        for h in (0, 1):
            cols = pl.ds(h * TILE, TILE)

            def block(i, carry):
                total = share2[direction, at, i, :, cols].astype(f32)
                for side in (0, 1):
                    total = total + final1[direction, side, i, :, cols].astype(f32)
                row_sum[direction, h, i] = total.astype(bf16)
                return carry

            lax.fori_loop(0, 4, block, 0)
            near_start(direction, h)

    def near_mid(direction, h):
        col_near[direction][h].mid(1)
        col_near[direction][h].mid(-1)

    stores = []

    def sum_near(direction):
        for h in (0, 1):
            col_near[direction][h].end()
            total = row_sum[direction, h, near_me(direction)].astype(f32)
            for side in (0, 1):
                total = total + final2[direction, h, side].astype(f32)
            total = total + passing2[direction, h].reshape(32, TILE).astype(f32)
            out_buf[direction, :, pl.ds(h * TILE, TILE)] = total.astype(bf16)
        store = pltpu.make_async_copy(out_buf.at[direction], (output, grad_tokens)[direction], store_sem.at[direction])
        store.start()
        stores.append(store)

    def grad_ready(which):
        for k in range(4):
            arrived(chunk(other.at[1 - which], 1 - which, place(1 - which, k)),
                    depth_s.at[1 - which, k], depth_r.at[1 - which, k])
            arrived(chunk(act_other.at[which], which, place(which, k)),
                    depth_s.at[which, 4 + k], depth_r.at[which, 4 + k])

    def weight_grad(which, first, last):
        half = pl.multiple_of(d * 768, 128)
        result = gw_out if which == FWD else gw_in
        target = grad_w_out if which == FWD else grad_w_in

        def tile(i, carry):
            start = pl.multiple_of(i * 256, 256)
            rows = pl.ds(start, 256)
            if which == FWD:
                lhs = act[FWD, :, :, :, pl.ds(half + start, 256)].reshape(512, 256)
                rhs = slabs[BWD].reshape(512, 1536)
                lhs_other = act_other[FWD, :, :, :, rows].reshape(512, 256)
                rhs_other = other[BWD].reshape(512, 1536)
            else:
                lhs = slabs[FWD, :, :, :, rows].reshape(512, 256)
                rhs = act[BWD, :, :, :, pl.ds(half, 768)].reshape(512, 768)
                lhs_other = other[FWD, :, :, :, rows].reshape(512, 256)
                rhs_other = act_other[BWD].reshape(512, 768)
            product = lax.dot_general(lhs, rhs, contract_first, preferred_element_type=f32)
            product = product + lax.dot_general(lhs_other, rhs_other, contract_first, preferred_element_type=f32)
            result[rows] = product.astype(bf16)
            return carry

        lax.fori_loop(first, last, tile, 0)
        rows = pl.ds(first * 256, (last - first) * 256)
        store = pltpu.make_async_copy(result.at[rows], target.at[rows], grad_sem.at[which, first])
        store.start()
        stores.append(store)

    F, B = FWD, BWD
    load_tok.wait()
    gather_near[F].start()
    load_cot.wait()
    gather_near[B].start()
    load_out.wait()
    turn(B, 2)
    turn(B, 1)
    load_in.wait()
    turn(F, 1)
    gather_far[F][0].start()
    gather_far[B][0].start()
    gather_near[F].mid()
    turn(B, 0)
    gather_near[B].neighbour(1)
    gather_near[B].neighbour(-1)
    gather_near[B].mid()
    gather_far[B][1].start()
    gather_far[B][2].start()
    gather_near[F].neighbour(1)
    gather_near[F].neighbour(-1)
    gather_far[F][1].start()
    gather_far[F][2].start()
    gather_near[F].end()
    to_sibling(F, 0)
    first_matmul(F, 0)
    gather_far[F][3].start()
    gather_far[F][0].mid()
    gather_near[B].end()
    to_sibling(B, 0)
    gather_far[B][3].start()
    first_matmul(B, 0)
    pass_on(F, 0)
    first_matmul(B, 1)
    gather_far[F][1].mid()
    first_matmul(F, 1)
    gather_far[F][2].mid()
    gather_far[B][3].mid()
    gather_far[F][3].mid()
    turn(F, 2)
    turn(F, 0)
    activate(F, 0)
    first_matmul(F, 2)
    gather_far[B][2].mid()
    gather_far[B][1].mid()
    first_matmul(F, 3)
    gather_far[B][0].mid()
    pass_on(F, 1)
    first_matmul(B, 3)
    pass_on(F, 2)
    pass_on(B, 1)
    activate(F, 1)
    pass_on(F, 3)
    pass_on(B, 3)
    first_matmul(B, 2)
    activate(F, 2)
    activate(F, 3)
    activate(B, 3)
    forward_on(F, 2)
    pass_on(B, 2)
    forward_on(F, 3)
    activate(B, 1)
    forward_on(B, 3)
    activate(B, 2)
    forward_on(B, 1)
    second_matmul(F, 2)
    forward_on(F, 1)
    second_matmul(B, 3)
    forward_on(B, 2)
    second_matmul(F, 3)
    pass_on(B, 0)
    second_matmul(B, 1)
    second_matmul(B, 2)
    forward_on(F, 0)
    second_matmul(F, 1)
    activate(B, 0)
    far_mid(F, 1)
    far_mid(B, -1)
    far_mid(B, 1)
    second_matmul(F, 0)
    far_mid(F, -1)
    forward_on(B, 0)
    grad_ready(F)
    weight_grad(F, 0, 2)
    second_matmul(B, 0)
    sum_far(F)
    weight_grad(F, 2, 3)
    grad_ready(B)
    weight_grad(B, 0, 2)
    sum_far(B)
    weight_grad(B, 2, 3)
    near_mid(B, 0)
    near_mid(F, 1)
    near_mid(F, 0)
    near_mid(B, 1)
    weight_grad(B, 3, 6)
    sum_near(B)
    sum_near(F)
    for copy in sent:
        copy.wait_send()
    for store in stores:
        store.wait()


def hand_on(*refs):
    for source, target in zip(refs[:4], refs[4:]):
        target[...] = source[...]


def body(tokens, w_in, w_out, cotangent):
    anywhere = pl.BlockSpec(memory_space=pl.ANY)
    dma = pltpu.SemaphoreType.DMA
    vmem = pltpu.VMEM
    results = pl.pallas_call(
        kernel,
        out_shape=(
            jax.ShapeDtypeStruct((32, 1536), bf16),
            jax.ShapeDtypeStruct((32, 1536), bf16),
            jax.ShapeDtypeStruct((1536, 768), bf16),
            jax.ShapeDtypeStruct((768, 1536), bf16),
        ),
        in_specs=[anywhere] * 4,
        out_specs=(anywhere,) * 4,
        scratch_shapes=[
            vmem((1536, 1536), bf16),
            vmem((1536, 1536), bf16),
            vmem((1536, 1536), bf16),
            vmem((1536, 1536), bf16),
            vmem((2, 4, 4, 32, 1536), bf16),
            vmem((2, 4, 4, 32, 1536), bf16),
            vmem((2, 4, 4, 32, 1536), bf16),
            vmem((2, 4, 2, 16, 1536), bf16),
            vmem((2, 4, 2, 32, 1536), bf16),
            vmem((4, 32, 1536), f32),
            vmem((2, 4, 4, 32, 1536), bf16),
            vmem((2, 4, 4, 32, 768), bf16),
            vmem((2, 4, 4, 32, 1536), bf16),
            vmem((2, 2, 2, 32, 1536), bf16),
            vmem((2, 2, 4, 32, 1536), bf16),
            vmem((2, 2, 4, 32, 768), bf16),
            vmem((2, 2, 2, 16, 768), bf16),
            vmem((2, 2, 2, 32, 768), bf16),
            vmem((2, 32, 1536), bf16),
            vmem((1536, 768), bf16),
            vmem((768, 1536), bf16),
            dma((4,)),
            dma((2, 5, 6)), dma((2, 5, 6)),
            dma((2, 4, 6)), dma((2, 4, 6)),
            dma((2, 4, 6)), dma((2, 4, 6)),
            dma((2, 8)), dma((2, 8)),
            dma((2, 3, 6)), dma((2, 3, 6)),
            dma((2,)),
            dma((2, 6)),
        ],
        compiler_params=pltpu.CompilerParams(
            collective_id=1, has_side_effects=True, vmem_limit_bytes=60 * 2**20
        ),
        cost_estimate=pl.CostEstimate(flops=14_500_000_000, bytes_accessed=15_000_000, transcendentals=0),
        name="ffn_block",
    )(tokens, w_in, w_out, cotangent)
    blocks = [pl.BlockSpec((r.shape[0] // 2, r.shape[1]), lambda i: (i, 0)) for r in results]
    return pl.pallas_call(
        hand_on,
        grid=(2,),
        out_shape=tuple(jax.ShapeDtypeStruct(r.shape, r.dtype) for r in results),
        in_specs=blocks,
        out_specs=tuple(blocks),
        compiler_params=pltpu.CompilerParams(vmem_limit_bytes=60 * 2**20),
        name="hand_on",
    )(*results)


def solution(mesh):
    in_specs = (
        P(("depth", "col"), "row"),
        P("row", "col"),
        P("col", "row"),
        P(("depth", "col"), "row"),
    )
    out_specs = (
        P(("depth", "col"), "row"),
        P(("depth", "col"), "row"),
        P("row", ("col", "depth")),
        P(("col", "depth"), "row"),
    )
    return jax.shard_map(body, mesh=mesh, in_specs=in_specs, out_specs=out_specs, check_vma=False)
```

```python
import jax
import jax.numpy as jnp
from jax import lax
from jax.experimental import pallas as pl
from jax.experimental.pallas import tpu as pltpu
from jax.sharding import PartitionSpec as P

MESH = pl.DeviceIdType.MESH
root_coeff = 0.7978845608028654
cubic_coeff = 0.044715
contract_first = (((0,), (0,)), ((), ()))
f32 = jnp.float32
bf16 = jnp.bfloat16
FWD, BWD = 0, 1
STEP = (0, 1, 3, 2)
TILE = 768


def gelu_value(pre_act):
    inner = root_coeff * (pre_act + cubic_coeff * pre_act * pre_act * pre_act)
    return 0.5 * pre_act * (1.0 + jnp.tanh(inner))


def gelu_slope(pre_act):
    squared = pre_act * pre_act
    tangent = jnp.tanh(root_coeff * (pre_act + cubic_coeff * squared * pre_act))
    return 0.5 * (1.0 + tangent) + 0.5 * pre_act * (1.0 - tangent * tangent) * root_coeff * (
        1.0 + 3.0 * cubic_coeff * squared
    )


def mod4(value):
    return lax.rem(value + 8, 4)


def kernel(
    tokens, w_in_hbm, w_out_hbm, cotangent,
    output, grad_tokens, grad_w_in, grad_w_out,
    w_in, w_out, w_in_t, w_out_t, slabs, other, share, passing, final, pre, act, act_other,
    share2, passing1, final1, row_sum, passing2, final2, out_buf, gw_in, gw_out,
    load_sem, gather_s, gather_r, scat_s, scat_r, spread_s, spread_r,
    depth_s, depth_r, col_s, col_r, store_sem, grad_sem,
):
    x = lax.axis_index("row")
    c = lax.axis_index("col")
    d = lax.axis_index("depth")
    z, y = c // 4, lax.rem(c, 4)
    left, right = mod4(x - 1), mod4(x + 1)
    axis_me = (z, y)

    def at_x(value):
        return {"row": value, "col": c, "depth": d}

    def at_z(value):
        return {"row": x, "col": value * 4 + y, "depth": d}

    def at_y(value):
        return {"row": x, "col": z * 4 + value, "depth": d}

    sibling = {"row": x, "col": c, "depth": 1 - d}

    def remote(src, dst, send, recv, device):
        return pltpu.make_async_remote_copy(
            src_ref=src, dst_ref=dst, send_sem=send, recv_sem=recv, device_id=device, device_id_type=MESH
        )

    sent = []

    def push(src, dst, send, recv, device):
        copy = remote(src, dst, send, recv, device)
        copy.start()
        sent.append(copy)

    def arrived(ref, send, recv):
        remote(ref, ref, send, recv, sibling).wait_recv()

    load_tok = pltpu.make_async_copy(tokens, slabs.at[FWD, z, y], load_sem.at[0])
    load_cot = pltpu.make_async_copy(cotangent, slabs.at[BWD, z, y], load_sem.at[1])
    load_in = pltpu.make_async_copy(w_in_hbm, w_in, load_sem.at[2])
    load_out = pltpu.make_async_copy(w_out_hbm, w_out, load_sem.at[3])
    for load in (load_tok, load_cot, load_in, load_out):
        load.start()

    barrier = pltpu.get_barrier_semaphore()
    peers = [at_x(left), at_x(right), sibling]
    for step in (1, 2, 3):
        peers += [at_z(mod4(z + step)), at_y(mod4(y + step))]
    for peer in peers:
        pl.semaphore_signal(barrier, inc=1, device_id=peer, device_id_type=MESH)
    pl.semaphore_wait(barrier, len(peers))

    def place(direction, k):
        return mod4(axis_me[direction] + STEP[k])

    def chunk(ref, direction, at):
        return ref.at[at] if direction == FWD else ref.at[:, at]

    def near(direction, value):
        return at_y(value) if direction == FWD else at_z(value)

    def far(direction, value):
        return at_z(value) if direction == FWD else at_y(value)

    def near_me(direction):
        return axis_me[1 - direction]

    def far_me(direction):
        return axis_me[direction]

    low_rows, high_rows = pl.ds(0, 16), pl.ds(16, 16)
    low_blocks, high_blocks = pl.ds(0, 2), pl.ds(2, 2)

    class Spread:
        def __init__(self, item, me, to, halves, send, recv, direct=False):
            self.direct = direct
            self.item, self.me, self.to, self.halves = item, me, to, halves
            self.send, self.recv = send, recv
            self.here = set()

        def need(self, n, offset, half):
            if n not in self.here:
                self.here.add(n)
                arrived(self.part(offset, half), self.send(n), self.recv(n))

        def part(self, offset, half):
            return self.item(mod4(self.me + offset)).at[self.halves[half]]

        def start(self):
            own, to = self.item(self.me), self.to
            for half, n, step in ((0, 0, 1), (1, 1, -1), (1, 2, 1), (0, 3, -1)):
                part = own.at[self.halves[half]]
                push(part, part, self.send(n), self.recv(n), to(mod4(self.me + step)))
            if self.direct:
                for half in (0, 1):
                    part = own.at[self.halves[half]]
                    push(part, part, self.send(4 + half), self.recv(4 + half), to(mod4(self.me + 2)))

        def mid(self):
            if self.direct:
                return
            for half, n, source, step in ((0, 0, -1, 1), (1, 1, 1, -1)):
                self.need(n, source, half)
                part = self.part(source, half)
                push(part, part, self.send(n + 4), self.recv(n + 4), self.to(mod4(self.me + step)))

        def neighbour(self, step):
            for n, half in ((1, 1), (3, 0)) if step == 1 else ((0, 0), (2, 1)):
                self.need(n, step, half)

        def end(self):
            self.need(4, 2, 0)
            self.need(5, 2, 1)

    class Scatter:
        def __init__(self, piece, me, to, halves, passing, final, send, recv, add, direct=False):
            self.direct = direct
            self.piece, self.me, self.to, self.halves = piece, me, to, halves
            self.passing, self.final, self.send, self.recv, self.add = passing, final, send, recv, add

        def start_far(self):
            piece = self.piece(mod4(self.me + 2))
            for half, step in ((0, 1), (1, -1)):
                push(piece.at[self.halves[half]], self.passing.at[half], self.send(half), self.recv(half),
                     self.to(mod4(self.me + (2 if self.direct else step))))

        def start_near(self, step):
            side = 0 if step == 1 else 1
            half = self.halves[1 - side]
            push(self.piece(mod4(self.me + step)).at[half], self.final.at[side, half],
                 self.send(2 + side), self.recv(2 + side), self.to(mod4(self.me + step)))
            if self.direct:
                half = self.halves[side]
                push(self.piece(mod4(self.me + step)).at[half], self.final.at[side, half],
                     self.send(4 + side), self.recv(4 + side), self.to(mod4(self.me + step)))

        def mid(self, step):
            if self.direct:
                return
            side = 0 if step == 1 else 1
            half = self.halves[side]
            arrived(self.passing.at[side], self.send(side), self.recv(side))
            mine = self.piece(mod4(self.me + step)).at[half]
            self.add(mine, self.passing.at[side])
            push(mine, self.final.at[side, half], self.send(4 + side), self.recv(4 + side),
                 self.to(mod4(self.me + step)))

        def end(self):
            if self.direct:
                for half in (0, 1):
                    arrived(self.passing.at[half], self.send(half), self.recv(half))
            for side in (0, 1):
                arrived(self.final.at[side, self.halves[1 - side]], self.send(2 + side), self.recv(2 + side))
            for side in (0, 1):
                arrived(self.final.at[side, self.halves[side]], self.send(4 + side), self.recv(4 + side))

    def add_rows(mine, more):
        mine[...] = (mine[...].astype(f32) + more[...].astype(f32)).astype(bf16)

    def add_blocks(mine, more):
        for i in range(2):
            add_rows(mine.at[i], more.at[i])

    def ring(ref, *where):
        return lambda n: ref.at[(*where, n)]

    gather_near, gather_far, col_far, col_near = [], [], [], []
    for direction in (FWD, BWD):
        def own_line(at, direction=direction):
            return chunk(slabs.at[direction], direction, far_me(direction)).at[at]

        def near_to(value, direction=direction):
            return near(direction, value)

        def far_to(value, direction=direction):
            return far(direction, value)

        def partial_chunk(at, direction=direction):
            return share2.at[direction, at]

        gather_near.append(Spread(own_line, near_me(direction), near_to, (low_rows, high_rows),
                                  ring(gather_s, direction, 0), ring(gather_r, direction, 0), True))
        lines = []
        for j in range(4):
            def far_line(at, direction=direction, block=mod4(near_me(direction) + STEP[j])):
                return chunk(slabs.at[direction], direction, at).at[block]

            lines.append(Spread(far_line, far_me(direction), far_to, (low_rows, high_rows),
                                ring(gather_s, direction, 1 + j), ring(gather_r, direction, 1 + j)))
        gather_far.append(lines)
        col_far.append(Scatter(partial_chunk, far_me(direction), far_to, (low_blocks, high_blocks),
                               passing1.at[direction], final1.at[direction],
                               ring(col_s, direction, 0), ring(col_r, direction, 0), add_blocks))
        halves = []
        for h in (0, 1):
            def summed_block(at, direction=direction, h=h):
                return row_sum.at[direction, h, at]

            halves.append(Scatter(summed_block, near_me(direction), near_to, (low_rows, high_rows),
                                  passing2.at[direction, h], final2.at[direction, h],
                                  ring(col_s, direction, 1 + h), ring(col_r, direction, 1 + h), add_rows, True))
        col_near.append(halves)

    def block_of(direction, at, owner):
        block = mod4(owner - at)
        return act.at[direction, at, block] if direction == FWD else act.at[direction, block, at]

    x_sum, x_spread = [[], []], [[], []]
    for direction in (FWD, BWD):
        for k in range(4):
            def piece(owner, direction=direction, at=place(direction, k)):
                return share.at[direction, at, mod4(owner - at)]

            def item(owner, direction=direction, at=place(direction, k)):
                return block_of(direction, at, owner)

            x_sum[direction].append(Scatter(
                piece, x, at_x, (low_rows, high_rows), passing.at[direction, k], final.at[direction, k],
                ring(scat_s, direction, k), ring(scat_r, direction, k), add_rows))
            x_spread[direction].append(Spread(
                item, x, at_x, (low_rows, high_rows), ring(spread_s, direction, k), ring(spread_r, direction, k)))

    def turn(direction, i):
        rows = pl.ds(i * 512, 512)
        if direction == FWD:
            w_in_t[:, rows] = w_in[rows, :].T
        else:
            w_out_t[:, rows] = w_out[rows, :].T

    far_mids, at_once = [0, 0], [False, False]

    def to_sibling(direction, k):
        at = place(direction, k)
        push(chunk(slabs.at[direction], direction, at), chunk(other.at[direction], direction, at),
             depth_s.at[direction, k], depth_r.at[direction, k], sibling)

    def first_matmul(direction, k):
        at = place(direction, k)
        for line in gather_far[direction]:
            if k == 1:
                line.neighbour(1)
            elif k == 2:
                line.neighbour(-1)
            elif k == 3:
                line.end()
        lhs = chunk(slabs.at[direction], direction, at)
        if k:
            to_sibling(direction, k)

        def tile(i, carry):
            cols = pl.ds(pl.multiple_of(i * TILE, TILE), TILE)
            rows = lhs[...].reshape(128, 1536)
            if direction == FWD:
                product = jnp.dot(rows, w_in[:, cols], preferred_element_type=f32)
            else:
                product = jnp.dot(rows, w_out_t[:, cols], preferred_element_type=f32)
            share[direction, at, :, :, cols] = product.astype(bf16).reshape(4, 32, TILE)
            return carry

        lax.fori_loop(0, 1536 // TILE, tile, 0)
        scatter = x_sum[direction][k]
        scatter.start_far()
        scatter.start_near(1)
        scatter.start_near(-1)

    def pass_on(direction, k):
        x_sum[direction][k].mid(1)
        x_sum[direction][k].mid(-1)

    def activate(direction, k):
        at = place(direction, k)
        x_sum[direction][k].end()
        block = mod4(x - at)
        mine = share.at[direction, at, block]
        place_z = at if direction == FWD else block
        result = block_of(direction, at, x)

        def rows(i, carry):
            part = pl.ds(pl.multiple_of(i * 16, 16), 16)
            total = mine[part].astype(f32)
            total = total + final[direction, k, 0, part].astype(f32)
            total = total + final[direction, k, 1, part].astype(f32)
            if direction == FWD:
                pre[place_z, part] = total
                result[part] = gelu_value(total).astype(bf16)
            else:
                result[part] = (total * gelu_slope(pre[place_z, part])).astype(bf16)
            return carry

        lax.fori_loop(0, 2, rows, 0)
        x_spread[direction][k].start()

    def forward_on(direction, k):
        x_spread[direction][k].mid()

    def second_matmul(direction, k):
        at = place(direction, k)
        x_spread[direction][k].neighbour(1)
        x_spread[direction][k].neighbour(-1)
        x_spread[direction][k].end()
        if k == 0 and far_mids[direction] == 2:
            col_far[direction].end()
            at_once[direction] = True
        lhs = chunk(act.at[direction], direction, at)
        half = pl.ds(pl.multiple_of((1 - d) * 768, 128), 768)
        push(lhs.at[:, :, half], chunk(act_other.at[direction], direction, at),
             depth_s.at[direction, 4 + k], depth_r.at[direction, 4 + k], sibling)

        def tile(i, carry):
            cols = pl.ds(pl.multiple_of(i * TILE, TILE), TILE)
            rows = lhs[...].reshape(128, 1536)
            if direction == FWD:
                product = jnp.dot(rows, w_out[:, cols], preferred_element_type=f32)
            else:
                product = jnp.dot(rows, w_in_t[:, cols], preferred_element_type=f32)
            if k == 0 and at_once[direction]:
                product = product.reshape(4, 32, TILE)
                for side in (0, 1):
                    product = product + final1[direction, side, :, :, cols].astype(f32)
                row_sum[direction, i] = product.astype(bf16)
                return carry
            share2[direction, at, :, :, cols] = product.astype(bf16).reshape(4, 32, TILE)
            return carry

        if k == 0 and at_once[direction]:
            for h in (0, 1):
                lax.fori_loop(h, h + 1, tile, 0)
                near_start(direction, h)
            return
        lax.fori_loop(0, 1536 // TILE, tile, 0)
        scatter = col_far[direction]
        if k == 3:
            scatter.start_far()
        elif k:
            scatter.start_near(1 if k == 1 else -1)

    def far_mid(direction, step):
        col_far[direction].mid(step)
        far_mids[direction] += 1

    def near_start(direction, h):
        col_near[direction][h].start_far()
        col_near[direction][h].start_near(1)
        col_near[direction][h].start_near(-1)

    def sum_far(direction):
        if at_once[direction]:
            return
        col_far[direction].end()
        at = place(direction, 0)
        for h in (0, 1):
            cols = pl.ds(h * TILE, TILE)

            def block(i, carry):
                total = share2[direction, at, i, :, cols].astype(f32)
                for side in (0, 1):
                    total = total + final1[direction, side, i, :, cols].astype(f32)
                row_sum[direction, h, i] = total.astype(bf16)
                return carry

            lax.fori_loop(0, 4, block, 0)
            near_start(direction, h)

    def near_mid(direction, h):
        col_near[direction][h].mid(1)
        col_near[direction][h].mid(-1)

    stores = []

    def sum_near(direction):
        for h in (0, 1):
            col_near[direction][h].end()
            total = row_sum[direction, h, near_me(direction)].astype(f32)
            for side in (0, 1):
                total = total + final2[direction, h, side].astype(f32)
            total = total + passing2[direction, h].reshape(32, TILE).astype(f32)
            out_buf[direction, :, pl.ds(h * TILE, TILE)] = total.astype(bf16)
        store = pltpu.make_async_copy(out_buf.at[direction], (output, grad_tokens)[direction], store_sem.at[direction])
        store.start()
        stores.append(store)

    def grad_ready(which):
        for k in range(4):
            arrived(chunk(other.at[1 - which], 1 - which, place(1 - which, k)),
                    depth_s.at[1 - which, k], depth_r.at[1 - which, k])
            arrived(chunk(act_other.at[which], which, place(which, k)),
                    depth_s.at[which, 4 + k], depth_r.at[which, 4 + k])

    def weight_grad(which, first, last):
        half = pl.multiple_of(d * 768, 128)
        result = gw_out if which == FWD else gw_in
        target = grad_w_out if which == FWD else grad_w_in

        def tile(i, carry):
            start = pl.multiple_of(i * 256, 256)
            rows = pl.ds(start, 256)
            if which == FWD:
                lhs = act[FWD, :, :, :, pl.ds(half + start, 256)].reshape(512, 256)
                rhs = slabs[BWD].reshape(512, 1536)
                lhs_other = act_other[FWD, :, :, :, rows].reshape(512, 256)
                rhs_other = other[BWD].reshape(512, 1536)
            else:
                lhs = slabs[FWD, :, :, :, rows].reshape(512, 256)
                rhs = act[BWD, :, :, :, pl.ds(half, 768)].reshape(512, 768)
                lhs_other = other[FWD, :, :, :, rows].reshape(512, 256)
                rhs_other = act_other[BWD].reshape(512, 768)
            product = lax.dot_general(lhs, rhs, contract_first, preferred_element_type=f32)
            product = product + lax.dot_general(lhs_other, rhs_other, contract_first, preferred_element_type=f32)
            result[rows] = product.astype(bf16)
            return carry

        lax.fori_loop(first, last, tile, 0)
        rows = pl.ds(first * 256, (last - first) * 256)
        store = pltpu.make_async_copy(result.at[rows], target.at[rows], grad_sem.at[which, first])
        store.start()
        stores.append(store)

    F, B = FWD, BWD
    load_tok.wait()
    gather_near[F].start()
    load_cot.wait()
    gather_near[B].start()
    load_out.wait()
    turn(B, 2)
    gather_far[B][0].start()
    turn(B, 1)
    load_in.wait()
    turn(F, 1)
    gather_far[F][0].start()
    gather_near[F].mid()
    turn(B, 0)
    gather_near[B].neighbour(1)
    gather_near[B].neighbour(-1)
    gather_near[B].mid()
    gather_far[B][1].start()
    gather_far[B][2].start()
    gather_near[F].neighbour(1)
    gather_near[F].neighbour(-1)
    gather_far[F][1].start()
    gather_far[F][2].start()
    gather_near[F].end()
    to_sibling(F, 0)
    first_matmul(F, 0)
    gather_far[F][3].start()
    gather_far[F][0].mid()
    gather_near[B].end()
    to_sibling(B, 0)
    gather_far[B][3].start()
    first_matmul(B, 0)
    pass_on(F, 0)
    first_matmul(B, 1)
    gather_far[F][1].mid()
    first_matmul(F, 1)
    gather_far[F][2].mid()
    gather_far[B][3].mid()
    gather_far[F][3].mid()
    turn(F, 2)
    turn(F, 0)
    activate(F, 0)
    first_matmul(F, 2)
    gather_far[B][2].mid()
    gather_far[B][1].mid()
    first_matmul(F, 3)
    gather_far[B][0].mid()
    pass_on(F, 1)
    first_matmul(B, 3)
    pass_on(F, 2)
    pass_on(B, 1)
    activate(F, 1)
    pass_on(F, 3)
    pass_on(B, 3)
    first_matmul(B, 2)
    activate(F, 2)
    activate(F, 3)
    activate(B, 3)
    forward_on(F, 2)
    pass_on(B, 2)
    forward_on(F, 3)
    activate(B, 1)
    forward_on(B, 3)
    activate(B, 2)
    forward_on(B, 1)
    second_matmul(F, 2)
    forward_on(F, 1)
    second_matmul(B, 3)
    forward_on(B, 2)
    second_matmul(F, 3)
    pass_on(B, 0)
    second_matmul(B, 1)
    second_matmul(B, 2)
    forward_on(F, 0)
    second_matmul(F, 1)
    activate(B, 0)
    far_mid(F, 1)
    far_mid(B, -1)
    far_mid(B, 1)
    second_matmul(F, 0)
    far_mid(F, -1)
    forward_on(B, 0)
    grad_ready(F)
    weight_grad(F, 0, 2)
    second_matmul(B, 0)
    sum_far(F)
    weight_grad(F, 2, 3)
    grad_ready(B)
    weight_grad(B, 0, 2)
    sum_far(B)
    weight_grad(B, 2, 3)
    near_mid(F, 1)
    near_mid(F, 0)
    near_mid(B, 1)
    weight_grad(B, 3, 4)
    near_mid(B, 0)
    weight_grad(B, 4, 6)
    sum_near(B)
    sum_near(F)
    for copy in sent:
        copy.wait_send()
    for store in stores:
        store.wait()


def hand_on(*refs):
    for source, target in zip(refs[:4], refs[4:]):
        target[...] = source[...]


def body(tokens, w_in, w_out, cotangent):
    anywhere = pl.BlockSpec(memory_space=pl.ANY)
    dma = pltpu.SemaphoreType.DMA
    vmem = pltpu.VMEM
    results = pl.pallas_call(
        kernel,
        out_shape=(
            jax.ShapeDtypeStruct((32, 1536), bf16),
            jax.ShapeDtypeStruct((32, 1536), bf16),
            jax.ShapeDtypeStruct((1536, 768), bf16),
            jax.ShapeDtypeStruct((768, 1536), bf16),
        ),
        in_specs=[anywhere] * 4,
        out_specs=(anywhere,) * 4,
        scratch_shapes=[
            vmem((1536, 1536), bf16),
            vmem((1536, 1536), bf16),
            vmem((1536, 1536), bf16),
            vmem((1536, 1536), bf16),
            vmem((2, 4, 4, 32, 1536), bf16),
            vmem((2, 4, 4, 32, 1536), bf16),
            vmem((2, 4, 4, 32, 1536), bf16),
            vmem((2, 4, 2, 16, 1536), bf16),
            vmem((2, 4, 2, 32, 1536), bf16),
            vmem((4, 32, 1536), f32),
            vmem((2, 4, 4, 32, 1536), bf16),
            vmem((2, 4, 4, 32, 768), bf16),
            vmem((2, 4, 4, 32, 1536), bf16),
            vmem((2, 2, 2, 32, 1536), bf16),
            vmem((2, 2, 4, 32, 1536), bf16),
            vmem((2, 2, 4, 32, 768), bf16),
            vmem((2, 2, 2, 16, 768), bf16),
            vmem((2, 2, 2, 32, 768), bf16),
            vmem((2, 32, 1536), bf16),
            vmem((1536, 768), bf16),
            vmem((768, 1536), bf16),
            dma((4,)),
            dma((2, 5, 6)), dma((2, 5, 6)),
            dma((2, 4, 6)), dma((2, 4, 6)),
            dma((2, 4, 6)), dma((2, 4, 6)),
            dma((2, 8)), dma((2, 8)),
            dma((2, 3, 6)), dma((2, 3, 6)),
            dma((2,)),
            dma((2, 6)),
        ],
        compiler_params=pltpu.CompilerParams(
            collective_id=1, has_side_effects=True, vmem_limit_bytes=60 * 2**20
        ),
        cost_estimate=pl.CostEstimate(flops=14_500_000_000, bytes_accessed=15_000_000, transcendentals=0),
        name="ffn_block",
    )(tokens, w_in, w_out, cotangent)
    blocks = [pl.BlockSpec((r.shape[0] // 2, r.shape[1]), lambda i: (i, 0)) for r in results]
    return pl.pallas_call(
        hand_on,
        grid=(2,),
        out_shape=tuple(jax.ShapeDtypeStruct(r.shape, r.dtype) for r in results),
        in_specs=blocks,
        out_specs=tuple(blocks),
        compiler_params=pltpu.CompilerParams(vmem_limit_bytes=60 * 2**20),
        name="hand_on",
    )(*results)


def solution(mesh):
    in_specs = (
        P(("depth", "col"), "row"),
        P("row", "col"),
        P("col", "row"),
        P(("depth", "col"), "row"),
    )
    out_specs = (
        P(("depth", "col"), "row"),
        P(("depth", "col"), "row"),
        P("row", ("col", "depth")),
        P(("col", "depth"), "row"),
    )
    return jax.shard_map(body, mesh=mesh, in_specs=in_specs, out_specs=out_specs, check_vma=False)
```
